256 devices in a mesh: space: 64 (over y, z_hi, x), mode: 4 (over z_lo, core).
Axes of the slice: x: 4, y: 4, z: 8 (z_hi: 4, z_lo: 2; z = z_hi * 2 + z_lo), core: 2. Of those that a mesh axis runs over, the one named last changes fastest.
Arguments:
- start_field: float32 [36, 128, 64, 128], P('mode', 'space'), may hold values from -1.8 to 1.8
- source: float32 [36, 128, 64, 128], P('mode', 'space')
- mean_field: float32 [128, 64, 128], P('space'), may hold values from 0.5 to 2
- kl_fields: float32 [4, 128, 64, 128], P(None, 'space'), may hold values from -1 to 1
- triples: int32 [156, 3], replicated, may hold values from 0 to 35, as said below
- coef: float32 [156], replicated, may hold values from 0.5 to 2
Outputs:
- smoothed: float32 [36, 128, 64, 128], P('mode', 'space')
- residual: float32 [36, 128, 64, 128], P('mode', 'space')
The draws below stay inside these ranges and needn't reach their ends.
Inputs may be any that keep to these rules, and one draw needn't show every extreme that they name: Rows of triples are distinct. Field 0 appears only in the rows (0, s, s), one for every slot s of the 36 slots; the other rows name a field 1 to 4 and two different slots.
All inputs are finite; a program needn't handle non-finite values.
Results may differ from the reference program's by a relative error of at most 0.00022.
Values sent between devices are 32-bit elements; how exact they have to be, the bound alone decides.
No kernel may reach another device: no remote copies, remote signals or barrier semaphores. Data moves between devices by JAX's collectives and lax.ppermute only.
A program may use at most 64 MiB of HBM per device.

```python
import math
import jax
import jax.numpy as jnp
import numpy as np
from jax import lax

VARS = 4
DEGREE = 3
KL = 5
PS = 36
NNZ = 156
NX = 64
NY = 128
NZ = 128


def hermite_pairs():
    multis = []
    for first in range(DEGREE + 1):
        for second in range(DEGREE + 1 - first):
            for third in range(DEGREE + 1 - first - second):
                for fourth in range(DEGREE + 1 - first - second - third):
                    multis.append((first, second, third, fourth))
    multis.sort(key=lambda item: (item[0] + item[1] + item[2] + item[3], item))
    lookup = {}
    for number, item in enumerate(multis):
        lookup[item] = number
    rows_out = []
    for item in multis:
        if item[0] + item[1] + item[2] + item[3] < DEGREE:
            for which in range(VARS):
                raised = list(item)
                raised[which] = raised[which] + 1
                other = lookup[tuple(raised)]
                rows_out.append((which, lookup[item], other))
                rows_out.append((which, other, lookup[item]))
    return np.array(rows_out, dtype=np.int32)


def draw_triples(key, part):
    table = jnp.asarray(hermite_pairs())
    slots = jax.random.permutation(key, PS).astype(jnp.int32)
    variables = jax.random.permutation(jax.random.fold_in(key, 7), VARS).astype(jnp.int32) + 1
    coupled = jnp.stack([variables[table[:, 0]], slots[table[:, 1]], slots[table[:, 2]]], axis=1)
    own_slots = jnp.arange(PS, dtype=jnp.int32)
    mean_rows = jnp.stack([jnp.zeros((PS,), jnp.int32), own_slots, own_slots], axis=1)
    return jnp.concatenate([mean_rows, coupled], axis=0).astype(jnp.int32)


def draw_source(key, part):
    shape = (PS, NZ, NX, NY)
    return jnp.clip(jax.random.normal(key, shape, jnp.float32), -6.0, 6.0)


def block_scale(stream_key, dims, cuts, low, high):
    level, own = 1.0, jax.random.fold_in(stream_key, 6)
    for axis_at, shards_of in cuts:
        draws = jnp.exp(jax.random.uniform(jax.random.fold_in(own, axis_at), (shards_of,), jnp.float32, low / len(cuts), high / len(cuts)))
        level = level * jnp.repeat(draws, dims[axis_at] // shards_of).reshape([-1 if axis == axis_at else 1 for axis in range(len(dims))])
    return level


def noise(own_key, dims, scale, reach, shards=(), kind=jnp.bfloat16):
    gain = block_scale(own_key, dims, shards, -0.22, 0.18) if shards else 1.0
    values = jax.random.normal(own_key, dims, jnp.float32) * scale * gain
    return jnp.minimum(jnp.maximum(values, -reach), reach).astype(kind)


def setup_inputs(seed: int = 0) -> dict:
    splits = jax.random.split(jax.random.key(seed), 7)
    start_field = noise(splits[0], (PS, NZ, NX, NY), 0.3, 1.8, ((0, 4), (1, 64)), jnp.float32)
    source = draw_source(jax.random.fold_in(splits[6], 71), 0)
    mean_field = jnp.clip(jnp.exp(math.log(2.0) - 1.3862944 * jax.random.uniform(splits[2], (NZ, NX, NY), jnp.float32) ** block_scale(splits[2], (NZ, NX, NY), ((0, 64),), -0.2, 0.2)), 0.5, 2.0)
    kl_fields = noise(splits[3], (VARS, NZ, NX, NY), 0.25, 1.0, ((1, 64),), jnp.float32)
    triples = draw_triples(jax.random.fold_in(splits[6], 71), 0)
    coef = jnp.clip(jnp.exp(jax.random.uniform(splits[5], (NNZ,), jnp.float32, math.log(0.5), math.log(2.0))), 0.5, 2.0)
    return dict(start_field=start_field, source=source, mean_field=mean_field, kl_fields=kl_fields, triples=triples, coef=coef)


def neighbour_views(arr):
    return [arr[..., 2:, 1:-1, 1:-1], arr[..., :-2, 1:-1, 1:-1],
            arr[..., 1:-1, 2:, 1:-1], arr[..., 1:-1, :-2, 1:-1],
            arr[..., 1:-1, 1:-1, 2:], arr[..., 1:-1, 1:-1, :-2]]


def stencil(field_pad, coeff_pad):
    centre = field_pad[..., 1:-1, 1:-1, 1:-1]
    own = coeff_pad[..., 1:-1, 1:-1, 1:-1]
    result = None
    for value, other in zip(neighbour_views(field_pad), neighbour_views(coeff_pad)):
        term = 0.5 * (own + other) * (centre - value)
        result = term if result is None else result + term
    return result


def face_total(coeff_pad):
    own = coeff_pad[..., 1:-1, 1:-1, 1:-1]
    result = None
    for other in neighbour_views(coeff_pad):
        term = 0.5 * (own + other)
        result = term if result is None else result + term
    return result


def reference(start_field, source, mean_field, kl_fields, triples, coef):
    coupling = jnp.zeros((KL, PS, PS), jnp.float32).at[triples[:, 0], triples[:, 1], triples[:, 2]].add(coef)
    fields = jnp.concatenate([mean_field[None], kl_fields], axis=0)
    coeff_pad = jnp.pad(fields, ((0, 0), (1, 1), (1, 1), (1, 1)))
    scaling = jnp.diagonal(coupling[0])[:, None, None, None] * face_total(coeff_pad[0])[None]
    per_row = jnp.transpose(coupling, (1, 0, 2))

    def operator(field):
        def one_mode(row):
            mixed = jnp.einsum('mj,jzxy->mzxy', row, field, precision=lax.Precision.HIGHEST)
            mixed_pad = jnp.pad(mixed, ((0, 0), (1, 1), (1, 1), (1, 1)))
            return jnp.sum(stencil(mixed_pad, coeff_pad), axis=0)
        return lax.map(one_mode, per_row)

    first = source - operator(start_field)
    middle = start_field + 0.8 * first / scaling
    residual = source - operator(middle)
    smoothed = middle + 0.8 * residual / scaling
    return smoothed, residual
```

```python
import functools

import jax
import jax.numpy as jnp
from jax import lax
from jax.experimental import pallas as pl
from jax.experimental.pallas import tpu as pltpu
from jax.sharding import PartitionSpec as P

LOCAL, ROWS, LANES, HELD = 9, 64, 128, 16
GROUPS = 4
SLOTS = LOCAL * GROUPS
FIELDS = 5
ENTRIES = 156
F32 = jnp.float32
VMEM = pl.BlockSpec(memory_space=pltpu.VMEM)
SMEM = pl.BlockSpec(memory_space=pltpu.SMEM)
ANY = pl.BlockSpec(memory_space=pl.ANY)
PARAMS = dict(compiler_params=pltpu.CompilerParams(vmem_limit_bytes=40 * 2**20))


def shape(*dims):
    return jax.ShapeDtypeStruct(dims, F32)


def cost(flops, nbytes):
    return pl.CostEstimate(flops=flops, bytes_accessed=nbytes, transcendentals=0)


def window(ref, lead, g, low, count):
    rows = ref[(*lead, pl.ds(pl.multiple_of(HELD * g, HELD), 32), slice(None))]
    return rows[..., 8 + low : 8 + low + count, :]


def fill_padded(src, padded, sem):
    copy = pltpu.make_async_copy(src, padded.at[..., pl.ds(8, ROWS), :], sem)
    copy.start()
    edge = jnp.zeros((*padded.shape[:-2], 8, LANES), F32)
    padded[..., 0:8, :] = edge
    padded[..., 8 + ROWS : 16 + ROWS, :] = edge
    return copy


def lane_next(x):
    lane = lax.broadcasted_iota(jnp.int32, x.shape, x.ndim - 1)
    return jnp.where(lane == LANES - 1, 0.0, pltpu.roll(x, LANES - 1, x.ndim - 1))


def lane_prev(x):
    lane = lax.broadcasted_iota(jnp.int32, x.shape, x.ndim - 1)
    return jnp.where(lane == 0, 0.0, pltpu.roll(x, 1, x.ndim - 1))


def pack_start(g_ref, start, o0, o1, o2, o3, padded, sem):
    g = g_ref[0]
    fill_padded(start, padded, sem).wait()
    for d, out in enumerate((o0, o1, o2, o3)):
        for p in range(2):
            for k in range(LOCAL):
                at = k * 40 + 20 * p
                out[at : at + 20, :] = window(padded, (k, p), g ^ d, -2, 20)


def pack_source(g_ref, source, mean, kl, o0, o1, o2, o3, low, high, padded, klp, sems):
    g = g_ref[0]
    one = fill_padded(source, padded, sems.at[0])
    two = fill_padded(kl, klp, sems.at[1])
    three = pltpu.make_async_copy(mean.at[0], low.at[pl.ds(0, ROWS), :], sems.at[2])
    four = pltpu.make_async_copy(mean.at[1], high.at[pl.ds(0, ROWS), :], sems.at[3])
    three.start()
    four.start()
    two.wait()
    for p, out in enumerate((low, high)):
        for m in range(FIELDS - 1):
            at = ROWS + 18 * m
            out[at : at + 18, :] = window(klp, (m, p), g, -1, 18)
    one.wait()
    for d, out in enumerate((o0, o1, o2, o3)):
        for p in range(2):
            for k in range(LOCAL):
                at = k * 36 + 18 * p
                out[at : at + 18, :] = window(padded, (k, p), g ^ d, -1, 18)
    three.wait()
    four.wait()


def pack_edges(s0, s1, s2, s3, low, high):
    for d, src in enumerate((s0, s1, s2, s3)):
        for k in range(LOCAL):
            at = 18 * (LOCAL * d + k)
            low[at : at + 18, :] = src[k * 40 + 1 : k * 40 + 19, :]
            high[at : at + 18, :] = src[k * 40 + 21 : k * 40 + 39, :]


def accumulate(trip, cf, acc, count, faces, views):
    acc[...] = jnp.zeros(acc.shape, F32)

    def step(e, carry):
        m, i, j = trip[e], trip[ENTRIES + e], trip[2 * ENTRIES + e]
        c = cf[e]
        for p in range(2):
            total = None
            for b, view in enumerate(views(j, p)):
                term = faces[m, b, p] * view
                total = term if total is None else total + term
            acc[i, p] += c * total
        return carry

    lax.fori_loop(0, count, step, 0, unroll=2)


def first_sweep(
    trip, cf, g_ref, s0, s1, s2, s3, t0, t1, t2, t3, mean, kl, fl, fh, zl, zh,
    mid, b0, b1, b2, b3, low, high, faces_out,
    klp, ae, faces, vv, nxt, prv, acc, sems,
):
    g = g_ref[0]
    one = fill_padded(mean, klp.at[0], sems.at[0])
    two = fill_padded(kl, klp.at[pl.ds(1, FIELDS - 1)], sems.at[1])
    for d, src in enumerate((s0, s1, s2, s3)):
        for k in range(LOCAL):
            pos = LOCAL * d + k
            vv[pos, 0, 8:26, :] = zl[18 * pos : 18 * pos + 18, :]
            vv[pos, 3, 8:26, :] = zh[18 * pos : 18 * pos + 18, :]
            for p in range(2):
                vv[pos, 1 + p, 7:27, :] = src[k * 40 + 20 * p : k * 40 + 20 * p + 20, :]
                mine = vv[pos, 1 + p, 8:32, :]
                nxt[pos, p] = lane_next(mine)
                prv[pos, p] = lane_prev(mine)
    one.wait()
    two.wait()
    for m in range(FIELDS):
        for p in range(2):
            ae[m, 1 + p, 7:27, :] = window(klp, (m, p), g, -2, 20)
    for m in range(FIELDS - 1):
        at = ROWS + 18 * m
        ae[1 + m, 0, 8:26, :] = fl[at : at + 18, :]
        ae[1 + m, 3, 8:26, :] = fh[at : at + 18, :]
    for src, plane in ((fl, 0), (fh, 3)):
        klp[0, 0, 8 : 8 + ROWS, :] = src[0:ROWS, :]
        ae[0, plane, 8:26, :] = window(klp, (0, 0), g, -1, 18)
    for m in range(FIELDS):
        for p in range(2):
            own = ae[m, 1 + p, 8:32, :]
            others = (
                ae[m, 2 + p, 8:32, :], ae[m, p, 8:32, :],
                ae[m, 1 + p, 9:33, :], ae[m, 1 + p, 7:31, :],
                lane_next(own), lane_prev(own),
            )
            total = None
            for b, other in enumerate(others):
                face = 0.5 * (own + other)
                total = face if total is None else total + face
                faces[m, 1 + b, p] = -face
                faces_out[m, 1 + b, p] = -face[1 : 1 + HELD]
            faces[m, 0, p] = total
            faces_out[m, 0, p] = total[1 : 1 + HELD]

    def views(j, p):
        return (
            vv[j, 1 + p, 8:32, :], vv[j, 2 + p, 8:32, :], vv[j, p, 8:32, :],
            vv[j, 1 + p, 9:33, :], vv[j, 1 + p, 7:31, :], nxt[j, p], prv[j, p],
        )

    accumulate(trip, cf, acc, ENTRIES, faces, views)
    row = HELD * g - 1 + lax.broadcasted_iota(jnp.int32, (18, LANES), 0)
    inside = (row >= 0) & (row < ROWS)
    for p in range(2):
        rate = 0.8 / faces[0, 0, p, 0:18, :]
        for d, (src, out) in enumerate(((t0, b0), (t1, b1), (t2, b2), (t3, b3))):
            for k in range(LOCAL):
                pos = LOCAL * d + k
                at = k * 36 + 18 * p
                first = src[at : at + 18, :] - acc[pos, p, 0:18, :]
                moved = vv[pos, 1 + p, 8:26, :] + first * rate * cf[ENTRIES + pos]
                moved = jnp.where(inside, moved, 0.0)
                mid[pos, p, 7:25, :] = moved
                held = moved[1 : 1 + HELD]
                out[k, p] = held
                (low, high)[p][pos] = held


def second_residual(
    trip, cf, t0, t1, t2, t3, mid, faces, zl, zh, o0, o1, o2, o3, nxt, prv, acc
):
    for pos in range(SLOTS):
        for p in range(2):
            mine = mid[pos, p, 8:24, :]
            nxt[pos, p] = lane_next(mine)
            prv[pos, p] = lane_prev(mine)

    def views(j, p):
        return (
            mid[j, p, 8:24, :],
            zh[j] if p else mid[j, 1, 8:24, :],
            mid[j, 0, 8:24, :] if p else zl[j],
            mid[j, p, 9:25, :], mid[j, p, 7:23, :], nxt[j, p], prv[j, p],
        )

    accumulate(trip, cf, acc, ENTRIES, faces, views)
    for d, (src, out) in enumerate(((t0, o0), (t1, o1), (t2, o2), (t3, o3))):
        for k in range(LOCAL):
            for p in range(2):
                at = k * 36 + 18 * p + 1
                out[k, p] = src[at : at + HELD, :] - acc[LOCAL * d + k, p]


def second_sweep(
    cf, g_ref, mean, fl, fh, m0, m1, m2, m3, r0, r1, r2, r3, smoothed, residual, rate, pad
):
    g = g_ref[0]
    pad[0:8, :] = jnp.zeros((8, LANES), F32)
    pad[8 + ROWS :, :] = jnp.zeros((8, LANES), F32)
    for p in range(2):
        own = mean[p]
        pad[8 : 8 + ROWS, :] = own
        others = (
            fh[0:ROWS, :] if p else mean[1],
            mean[0] if p else fl[0:ROWS, :],
            pad[9 : 9 + ROWS, :], pad[7 : 7 + ROWS, :],
            lane_next(own), lane_prev(own),
        )
        total = None
        for other in others:
            face = 0.5 * (own + other)
            total = face if total is None else total + face
        rate[p] = 0.8 / total
    for d, (mid, res) in enumerate(((m0, r0), (m1, r1), (m2, r2), (m3, r3))):
        rows = pl.ds(pl.multiple_of(HELD * (g ^ d), HELD), HELD)
        for p in range(2):
            here = rate[p, rows, :]
            for k in range(LOCAL):
                left = res[k, p]
                residual[k, p, rows, :] = left
                smoothed[k, p, rows, :] = mid[k, p] + left * here * cf[ENTRIES + k]


def body(start_field, source, mean_field, kl_fields, triples, coef):
    g = lax.axis_index("mode")
    gs = g.astype(jnp.int32).reshape(1)
    modes = triples[:, 1:]
    at = LOCAL * ((modes // LOCAL) ^ g) + modes % LOCAL
    trip = jnp.concatenate([triples[:, 0], at[:, 0], at[:, 1]])
    diag = jnp.sum(
        jnp.where(
            (triples[:, 0:1] == 0) & (at[:, 0:1] == jnp.arange(SLOTS)[None]), coef[:, None], 0.0
        ),
        axis=0,
    )
    cf = jnp.concatenate([coef, 1.0 / diag])

    count = lax.axis_size("space")
    forward = [(i, i + 1) for i in range(count - 1)]
    backward = [(b, a) for a, b in forward]

    def up(x):
        return lax.ppermute(x, "space", forward)

    def down(x):
        return lax.ppermute(x, "space", backward)

    def trade(parts):
        return [parts[0]] + [
            lax.ppermute(parts[d], "mode", [(i, i ^ d) for i in range(GROUPS)])
            for d in range(1, GROUPS)
        ]

    sends = pl.pallas_call(
        pack_start,
        out_shape=[shape(360, LANES)] * 4,
        in_specs=[SMEM, ANY],
        out_specs=[VMEM] * 4,
        scratch_shapes=[pltpu.VMEM((LOCAL, 2, ROWS + 16, LANES), F32), pltpu.SemaphoreType.DMA],
        name="pack_start",
        **PARAMS,
    )(gs, start_field)
    starts = trade(sends)
    *sources, field_low, field_high = pl.pallas_call(
        pack_source,
        out_shape=[shape(324, LANES)] * 4 + [shape(136, LANES)] * 2,
        in_specs=[SMEM, ANY, ANY, ANY],
        out_specs=[VMEM] * 6,
        scratch_shapes=[
            pltpu.VMEM((LOCAL, 2, ROWS + 16, LANES), F32),
            pltpu.VMEM((FIELDS - 1, 2, ROWS + 16, LANES), F32),
            pltpu.SemaphoreType.DMA((4,)),
        ],
        name="pack_source",
        **PARAMS,
    )(gs, source, mean_field, kl_fields)
    below, above = up(field_high), down(field_low)
    sources = trade(sources)
    low, high = pl.pallas_call(
        pack_edges,
        out_shape=[shape(18 * SLOTS, LANES)] * 2,
        in_specs=[VMEM] * 4,
        out_specs=[VMEM] * 2,
        name="pack_edges",
        **PARAMS,
    )(*starts)
    zl, zh = up(high), down(low)
    mid, *mids, low, high, faces = pl.pallas_call(
        first_sweep,
        out_shape=[shape(SLOTS, 2, 32, LANES)]
        + [shape(LOCAL, 2, HELD, LANES)] * 4
        + [shape(SLOTS, HELD, LANES)] * 2
        + [shape(FIELDS, 7, 2, HELD, LANES)],
        in_specs=[SMEM] * 3 + [VMEM] * 8 + [ANY] * 2 + [VMEM] * 4,
        out_specs=[VMEM] * 8,
        scratch_shapes=[
            pltpu.VMEM((FIELDS, 2, ROWS + 16, LANES), F32),
            pltpu.VMEM((FIELDS, 4, 40, LANES), F32),
            pltpu.VMEM((FIELDS, 7, 2, 24, LANES), F32),
            pltpu.VMEM((SLOTS, 4, 40, LANES), F32),
            pltpu.VMEM((SLOTS, 2, 24, LANES), F32),
            pltpu.VMEM((SLOTS, 2, 24, LANES), F32),
            pltpu.VMEM((SLOTS, 2, 24, LANES), F32),
            pltpu.SemaphoreType.DMA((2,)),
        ],
        name="first_sweep",
        **PARAMS,
    )(trip, cf, gs, *starts, *sources, mean_field, kl_fields, below, above, zl, zh)
    zl, zh = up(high), down(low)
    mids = trade(mids)
    lefts = pl.pallas_call(
        second_residual,
        out_shape=[shape(LOCAL, 2, HELD, LANES)] * 4,
        in_specs=[SMEM] * 2 + [VMEM] * 8,
        out_specs=[VMEM] * 4,
        scratch_shapes=[pltpu.VMEM((SLOTS, 2, HELD, LANES), F32)] * 3,
        name="second_residual",
        **PARAMS,
    )(trip, cf, *sources, mid, faces, zl, zh)
    lefts = trade(lefts)
    smoothed, residual = pl.pallas_call(
        second_sweep,
        out_shape=[shape(LOCAL, 2, ROWS, LANES)] * 2,
        in_specs=[SMEM] * 2 + [VMEM] * 11,
        out_specs=[VMEM] * 2,
        scratch_shapes=[
            pltpu.VMEM((2, ROWS, LANES), F32),
            pltpu.VMEM((ROWS + 16, LANES), F32),
        ],
        name="second_sweep",
        **PARAMS,
    )(cf, gs, mean_field, below, above, *mids, *lefts)
    return (smoothed, residual)


def solution(mesh):
    return jax.shard_map(
        body,
        mesh=mesh,
        in_specs=(
            P("mode", "space", None, None),
            P("mode", "space", None, None),
            P("space", None, None),
            P(None, "space", None, None),
            P(),
            P(),
        ),
        out_specs=(P("mode", "space", None, None), P("mode", "space", None, None)),
        check_vma=False,
    )
```

```python
import functools

import jax
import jax.numpy as jnp
from jax import lax
from jax.experimental import pallas as pl
from jax.experimental.pallas import tpu as pltpu
from jax.sharding import PartitionSpec as P

LOCAL, ROWS, LANES, HELD = 9, 64, 128, 16
GROUPS = 4
SLOTS = LOCAL * GROUPS
FIELDS = 5
ENTRIES = 156
EDGE = 18 * SLOTS
EDGE_FIELDS = ROWS + 18 * (FIELDS - 1)
RELAY_FIRST, RELAY_SECOND = True, True
NEAR = 2 * LOCAL
F32 = jnp.float32
VMEM = pl.BlockSpec(memory_space=pltpu.VMEM)
SMEM = pl.BlockSpec(memory_space=pltpu.SMEM)
HBM = pl.BlockSpec(memory_space=pltpu.HBM)
COST = pl.CostEstimate(flops=20_000_000, bytes_accessed=12_000_000, transcendentals=0)
PARAMS = dict(compiler_params=pltpu.CompilerParams(vmem_limit_bytes=40 * 2**20))


def shape(*dims):
    return jax.ShapeDtypeStruct(dims, F32)


def window(ref, lead, g, low, count):
    rows = ref[(*lead, pl.ds(pl.multiple_of(HELD * g, HELD), 32), slice(None))]
    return rows[..., 8 + low : 8 + low + count, :]


def fill_padded(src, padded, sem):
    copy = pltpu.make_async_copy(src, padded.at[..., pl.ds(8, ROWS), :], sem)
    copy.start()
    edge = jnp.zeros((*padded.shape[:-2], 8, LANES), F32)
    padded[..., 0:8, :] = edge
    padded[..., 8 + ROWS : 16 + ROWS, :] = edge
    return copy


def lane_next(x):
    lane = lax.broadcasted_iota(jnp.int32, x.shape, x.ndim - 1)
    return jnp.where(lane == LANES - 1, 0.0, pltpu.roll(x, LANES - 1, x.ndim - 1))


def lane_prev(x):
    lane = lax.broadcasted_iota(jnp.int32, x.shape, x.ndim - 1)
    return jnp.where(lane == 0, 0.0, pltpu.roll(x, 1, x.ndim - 1))


def pack_start(ids, start, o0, o1, o2, o3, padded, sem):
    g = ids[0]
    fill_padded(start, padded, sem).wait()
    for d, out in enumerate((o0, o1, o2, o3)):
        for p in range(2):
            for k in range(LOCAL):
                at = k * 40 + 20 * p
                out[at : at + 20, :] = window(padded, (k, p), g ^ d, -2, 20)


def pack_fields(ids, mean, kl, even, odd, klp, sems):
    g, parity = ids[0], ids[1]
    two = fill_padded(kl, klp, sems.at[0])
    edges = []
    for out, plane, sem in ((even, 1 - parity, 1), (odd, parity, 2)):
        edges.append(
            pltpu.make_async_copy(mean.at[plane], out.at[pl.ds(0, ROWS), :], sems.at[sem])
        )
        edges[-1].start()
    two.wait()
    for out, plane in ((even, 1 - parity), (odd, parity)):
        for m in range(FIELDS - 1):
            at = ROWS + 18 * m
            out[at : at + 18, :] = window(klp, (m, plane), g, -1, 18)
    for edge in edges:
        edge.wait()


def pack_source(ids, source, o0, o1, o2, o3, padded, sem):
    g = ids[0]
    fill_padded(source, padded, sem).wait()
    for d, out in enumerate((o0, o1, o2, o3)):
        for p in range(2):
            for k in range(LOCAL):
                at = k * 36 + 18 * p
                out[at : at + 18, :] = window(padded, (k, p), g ^ d, -1, 18)


def edge(src, k, top, upward):
    low = src[k * 40 + 1 : k * 40 + 19, :]
    high = src[k * 40 + 21 : k * 40 + 39, :]
    return jnp.where(top == upward, high, low)


def pack_near(ids, s0, s1, odd):
    top = ids[1] == 0
    for d, src in enumerate((s0, s1)):
        for k in range(LOCAL):
            at = 18 * (LOCAL * d + k)
            odd[at : at + 18, :] = edge(src, k, top, False)


def pack_far(ids, s0, s1, s2, s3, field_even, field_odd, even, odd):
    top = ids[1] == 0
    for d, src in enumerate((s0, s1, s2, s3)):
        for k in range(LOCAL):
            pos = LOCAL * d + k
            even[18 * pos : 18 * pos + 18, :] = edge(src, k, top, True)
            if pos >= NEAR:
                at = 18 * (pos - NEAR)
                odd[at : at + 18, :] = edge(src, k, top, False)
    even[EDGE:, :] = field_even[...]
    odd[EDGE // 2 :, :] = field_odd[...]


def sides(ids, from_even, from_odd):
    top = ids[1] == 0
    return jnp.where(top, from_odd, from_even), jnp.where(top, from_even, from_odd)


def near_odd(ids, straight, relayed):
    return straight if relayed is None else jnp.where(ids[2] == 1, relayed, straight)


def accumulate(trip, cf, acc, term):
    def step(e, carry):
        m, i, j = trip[e], trip[ENTRIES + e], trip[2 * ENTRIES + e]
        c = cf[e]
        for p in range(2):
            acc[i, p] += c * term(m, j, p)
        return carry

    lax.fori_loop(0, ENTRIES, step, 0, unroll=2)


def first_inner(
    trip, cf, ids, s0, s1, s2, s3, mean, kl, acc, faces, klp, ae, vv, nxt, prv, sems
):
    g = ids[0]
    one = fill_padded(mean, klp.at[0], sems.at[0])
    two = fill_padded(kl, klp.at[pl.ds(1, FIELDS - 1)], sems.at[1])
    for d, src in enumerate((s0, s1, s2, s3)):
        for k in range(LOCAL):
            pos = LOCAL * d + k
            for p in range(2):
                vv[pos, p, 7:27, :] = src[k * 40 + 20 * p : k * 40 + 20 * p + 20, :]
                mine = vv[pos, p, 8:32, :]
                nxt[pos, p] = lane_next(mine)
                prv[pos, p] = lane_prev(mine)
    one.wait()
    two.wait()
    for m in range(FIELDS):
        for p in range(2):
            ae[m, p, 7:27, :] = window(klp, (m, p), g, -2, 20)
    for m in range(FIELDS):
        for p in range(2):
            own = ae[m, p, 8:32, :]
            others = (
                ae[m, 1 - p, 8:32, :],
                ae[m, p, 9:33, :], ae[m, p, 7:31, :],
                lane_next(own), lane_prev(own),
            )
            total = None
            for b, other in enumerate(others):
                face = 0.5 * (own + other)
                total = face if total is None else total + face
                faces[m, 2 + b, p] = -face
            faces[m, 0, p] = total
            faces[m, 1, p] = own
    acc[...] = jnp.zeros(acc.shape, F32)

    def term(m, j, p):
        total = faces[m, 0, p] * vv[j, p, 8:32, :] + faces[m, 2, p] * vv[j, 1 - p, 8:32, :]
        total += faces[m, 3, p] * vv[j, p, 9:33, :] + faces[m, 4, p] * vv[j, p, 7:31, :]
        return total + (faces[m, 5, p] * nxt[j, p] + faces[m, 6, p] * prv[j, p])

    accumulate(trip, cf, acc, term)


def first_outer(
    trip, cf, ids, inner, faces, *rest
):
    relayed, rest = (rest[0], rest[1:]) if RELAY_FIRST else (None, rest)
    s0, s1, s2, s3, t0, t1, t2, t3, near, far, ev = rest[:11]
    mid, b0, b1, b2, b3, even, odd_a, odd_b, outer, acc, zz, pad = rest[11:]
    g, top = ids[0], ids[1] == 0
    for m in range(FIELDS):
        at = ROWS + 18 * (m - 1)
        rows = slice(at, at + 18) if m else slice(0, ROWS)
        e = ev[EDGE + rows.start : EDGE + rows.stop, :]
        o = far[EDGE // 2 + rows.start : EDGE // 2 + rows.stop, :]
        for p, other in enumerate(sides(ids, e, o)):
            if m == 0:
                pad[0:8, :] = jnp.zeros((8, LANES), F32)
                pad[8 : 8 + ROWS, :] = other
                pad[8 + ROWS :, :] = jnp.zeros((8, LANES), F32)
                other = window(pad, (), g, -1, 18)
            outer[m, p, 0:18, :] = 0.5 * (faces[m, 1, p, 0:18, :] + other)
    for d, src in enumerate((s0, s1, s2, s3)):
        for k in range(LOCAL):
            pos = LOCAL * d + k
            rows = slice(18 * pos, 18 * pos + 18)
            if pos < NEAR:
                o = near_odd(ids, near[rows, :], None if relayed is None else relayed[rows, :])
            else:
                o = far[18 * (pos - NEAR) : 18 * (pos - NEAR) + 18, :]
            for p, z in enumerate(sides(ids, ev[rows, :], o)):
                at = k * 40 + 20 * p + 1
                zz[pos, p, 0:18, :] = src[at : at + 18, :] - z
    acc[...] = inner[...]
    accumulate(trip, cf, acc, lambda m, j, p: outer[m, p] * zz[j, p])
    row = HELD * g - 1 + lax.broadcasted_iota(jnp.int32, (18, LANES), 0)
    inside = (row >= 0) & (row < ROWS)
    rates = [0.8 / (faces[0, 0, p, 0:18, :] + outer[0, p, 0:18, :]) for p in range(2)]
    for d, (start, src, out) in enumerate(
        ((s0, t0, b0), (s1, t1, b1), (s2, t2, b2), (s3, t3, b3))
    ):
        for k in range(LOCAL):
            pos = LOCAL * d + k
            helds = []
            for p in range(2):
                at = k * 36 + 18 * p
                first = src[at : at + 18, :] - acc[pos, p, 0:18, :]
                at = k * 40 + 20 * p + 1
                moved = start[at : at + 18, :] + first * rates[p] * cf[ENTRIES + pos]
                moved = jnp.where(inside, moved, 0.0)
                mid[pos, p, 7:25, :] = moved
                held = moved[1 : 1 + HELD]
                out[k, p] = held
                helds.append(held)
            even[pos] = jnp.where(top, helds[1], helds[0])
            (odd_a if pos < NEAR else odd_b)[pos % NEAR] = jnp.where(top, helds[0], helds[1])


def second_inner(trip, cf, mid, faces, acc, nxt, prv):
    for pos in range(SLOTS):
        for p in range(2):
            mine = mid[pos, p, 8:24, :]
            nxt[pos, p] = lane_next(mine)
            prv[pos, p] = lane_prev(mine)
    acc[...] = jnp.zeros(acc.shape, F32)
    held = slice(1, 1 + HELD)

    def term(m, j, p):
        total = faces[m, 0, p, held] * mid[j, p, 8:24, :]
        total += faces[m, 2, p, held] * mid[j, 1 - p, 8:24, :]
        total += faces[m, 3, p, held] * mid[j, p, 9:25, :] + faces[m, 4, p, held] * mid[j, p, 7:23, :]
        return total + (faces[m, 5, p, held] * nxt[j, p] + faces[m, 6, p, held] * prv[j, p])

    accumulate(trip, cf, acc, term)


def second_outer(trip, cf, ids, inner, outer, mid, *rest):
    relayed, rest = (rest[0], rest[1:]) if RELAY_SECOND else (None, rest)
    t0, t1, t2, t3, near, far, ev, o0, o1, o2, o3, acc, zz = rest
    for pos in range(SLOTS):
        if pos < NEAR:
            o = near_odd(ids, near[pos], None if relayed is None else relayed[pos])
        else:
            o = far[pos - NEAR]
        for p, z in enumerate(sides(ids, ev[pos], o)):
            zz[pos, p] = mid[pos, p, 8:24, :] - z
    acc[...] = inner[...]
    accumulate(trip, cf, acc, lambda m, j, p: outer[m, p, slice(1, 1 + HELD)] * zz[j, p])
    for d, (src, out) in enumerate(((t0, o0), (t1, o1), (t2, o2), (t3, o3))):
        for k in range(LOCAL):
            for p in range(2):
                at = k * 36 + 18 * p + 1
                out[k, p] = src[at : at + HELD, :] - acc[LOCAL * d + k, p]


def second_sweep(
    cf, ids, mean, far, ev, m0, m1, m2, m3, r0, r1, r2, r3, smoothed, residual, rate, pad
):
    g = ids[0]
    below, above = sides(ids, ev[EDGE : EDGE + ROWS, :], far[EDGE // 2 : EDGE // 2 + ROWS, :])
    pad[0:8, :] = jnp.zeros((8, LANES), F32)
    pad[8 + ROWS :, :] = jnp.zeros((8, LANES), F32)
    for p in range(2):
        own = mean[p]
        pad[8 : 8 + ROWS, :] = own
        others = (
            above if p else mean[1],
            mean[0] if p else below,
            pad[9 : 9 + ROWS, :], pad[7 : 7 + ROWS, :],
            lane_next(own), lane_prev(own),
        )
        total = None
        for other in others:
            face = 0.5 * (own + other)
            total = face if total is None else total + face
        rate[p] = 0.8 / total
    for d, (mid, res) in enumerate(((m0, r0), (m1, r1), (m2, r2), (m3, r3))):
        rows = pl.ds(pl.multiple_of(HELD * (g ^ d), HELD), HELD)
        for p in range(2):
            here = rate[p, rows, :]
            for k in range(LOCAL):
                left = res[k, p]
                residual[k, p, rows, :] = left
                smoothed[k, p, rows, :] = mid[k, p] + left * here * cf[ENTRIES + k]


def body(start_field, source, mean_field, kl_fields, triples, coef):
    g = lax.axis_index("mode").astype(jnp.int32)
    slab = lax.axis_index("space").astype(jnp.int32)
    ids = jnp.stack([g, slab % 2, ((slab % 4 == 0) | (slab % 4 == 3)).astype(jnp.int32)])
    modes = triples[:, 1:]
    at = LOCAL * ((modes // LOCAL) ^ g) + modes % LOCAL
    trip = jnp.concatenate([triples[:, 0], at[:, 0], at[:, 1]])
    diag = jnp.sum(
        jnp.where(
            (triples[:, 0:1] == 0) & (at[:, 0:1] == jnp.arange(SLOTS)[None]), coef[:, None], 0.0
        ),
        axis=0,
    )
    cf = jnp.concatenate([coef, 1.0 / diag])

    count = lax.axis_size("space")
    def both(pairs):
        return [pair for a, b in pairs for pair in ((a, b), (b, a))]

    evens = both([(i, i + 1) for i in range(0, count, 2)])
    odds = both([(i, i + 1) for i in range(1, count - 1, 2)])
    inner = [(i + 1, i + 2) for i in range(0, count, 4)]
    hops = both(inner + [(i, i + 3) for i in range(0, count, 4)])
    relay = [(i, i + 4) for i in range(0, count - 4, 4)]
    relay += [(i + 7, i + 3) for i in range(0, count - 4, 4)]

    def meet(x, pairs):
        return lax.ppermute(x, "space", pairs)

    def trade(parts):
        return [parts[0]] + [
            lax.ppermute(parts[d], "mode", [(i, i ^ d) for i in range(GROUPS)])
            for d in range(1, GROUPS)
        ]

    sends = pl.pallas_call(
        pack_start,
        out_shape=[shape(360, LANES)] * 4,
        in_specs=[SMEM, HBM],
        out_specs=[VMEM] * 4,
        scratch_shapes=[pltpu.VMEM((LOCAL, 2, ROWS + 16, LANES), F32), pltpu.SemaphoreType.DMA],
        name="pack_start",
        **PARAMS,
    )(ids, start_field)
    starts = trade(sends)
    fields = pl.pallas_call(
        pack_fields,
        out_shape=[shape(EDGE_FIELDS, LANES)] * 2,
        in_specs=[SMEM, HBM, HBM],
        out_specs=[VMEM] * 2,
        scratch_shapes=[
            pltpu.VMEM((FIELDS - 1, 2, ROWS + 16, LANES), F32),
            pltpu.SemaphoreType.DMA((3,)),
        ],
        name="pack_fields",
        **PARAMS,
    )(ids, mean_field, kl_fields)
    near = pl.pallas_call(
        pack_near,
        out_shape=shape(EDGE // 2, LANES),
        in_specs=[SMEM] + [VMEM] * 2,
        out_specs=VMEM,
        name="pack_near",
        **PARAMS,
    )(ids, *starts[:2])
    near = meet(near, hops if RELAY_FIRST else odds)
    even, odd = pl.pallas_call(
        pack_far,
        out_shape=[shape(EDGE + EDGE_FIELDS, LANES), shape(EDGE // 2 + EDGE_FIELDS, LANES)],
        in_specs=[SMEM] + [VMEM] * 6,
        out_specs=[VMEM] * 2,
        name="pack_far",
        **PARAMS,
    )(ids, *starts, *fields)
    edges = (near, meet(odd, odds), meet(even, evens))
    source, odd = lax.optimization_barrier((source, odd))
    sources = trade(pl.pallas_call(
        pack_source,
        out_shape=[shape(324, LANES)] * 4,
        in_specs=[SMEM, HBM],
        out_specs=[VMEM] * 4,
        scratch_shapes=[pltpu.VMEM((LOCAL, 2, ROWS + 16, LANES), F32), pltpu.SemaphoreType.DMA],
        name="pack_source",
        **PARAMS,
    )(ids, source))
    relayed = ()
    if RELAY_FIRST:
        near, sources[0] = lax.optimization_barrier((near, sources[0]))
        relayed = (meet(near, relay),)
    acc, faces = pl.pallas_call(
        first_inner,
        out_shape=[shape(SLOTS, 2, 24, LANES), shape(FIELDS, 7, 2, 24, LANES)],
        in_specs=[SMEM] * 3 + [VMEM] * 4 + [HBM] * 2,
        out_specs=[VMEM] * 2,
        scratch_shapes=[
            pltpu.VMEM((FIELDS, 2, ROWS + 16, LANES), F32),
            pltpu.VMEM((FIELDS, 2, 40, LANES), F32),
            pltpu.VMEM((SLOTS, 2, 40, LANES), F32),
            pltpu.VMEM((SLOTS, 2, 24, LANES), F32),
            pltpu.VMEM((SLOTS, 2, 24, LANES), F32),
            pltpu.SemaphoreType.DMA((2,)),
        ],
        cost_estimate=COST,
        name="first_inner",
        **PARAMS,
    )(trip, cf, ids, *starts, mean_field, kl_fields)
    operands = (trip, cf, ids, acc, faces, *relayed, *starts, *sources, *edges)
    mid, *mids, even, odd_a, odd_b, outer = pl.pallas_call(
        first_outer,
        out_shape=[shape(SLOTS, 2, 32, LANES)]
        + [shape(LOCAL, 2, HELD, LANES)] * 4
        + [shape(SLOTS, HELD, LANES)]
        + [shape(SLOTS // 2, HELD, LANES)] * 2
        + [shape(FIELDS, 2, 24, LANES)],
        in_specs=[SMEM] * 3 + [VMEM] * (len(operands) - 3),
        out_specs=[VMEM] * 9,
        scratch_shapes=[pltpu.VMEM((SLOTS, 2, 24, LANES), F32)] * 2
        + [pltpu.VMEM((ROWS + 16, LANES), F32)],
        name="first_outer",
        **PARAMS,
    )(*operands)
    near = meet(odd_a, hops if RELAY_SECOND else odds)
    met = (near, meet(odd_b, odds), meet(even, evens))
    relayed = (meet(near, relay),) if RELAY_SECOND else ()
    mids = trade(mids)
    acc = pl.pallas_call(
        second_inner,
        out_shape=shape(SLOTS, 2, HELD, LANES),
        in_specs=[SMEM] * 2 + [VMEM] * 2,
        out_specs=VMEM,
        scratch_shapes=[pltpu.VMEM((SLOTS, 2, HELD, LANES), F32)] * 2,
        cost_estimate=COST,
        name="second_inner",
        **PARAMS,
    )(trip, cf, mid, faces)
    operands = (trip, cf, ids, acc, outer, mid, *relayed, *sources, *met)
    lefts = pl.pallas_call(
        second_outer,
        out_shape=[shape(LOCAL, 2, HELD, LANES)] * 4,
        in_specs=[SMEM] * 3 + [VMEM] * (len(operands) - 3),
        out_specs=[VMEM] * 4,
        scratch_shapes=[pltpu.VMEM((SLOTS, 2, HELD, LANES), F32)] * 2,
        name="second_outer",
        **PARAMS,
    )(*operands)
    lefts = trade(lefts)
    smoothed, residual = pl.pallas_call(
        second_sweep,
        out_shape=[shape(LOCAL, 2, ROWS, LANES)] * 2,
        in_specs=[SMEM] * 2 + [VMEM] * 11,
        out_specs=[VMEM] * 2,
        scratch_shapes=[
            pltpu.VMEM((2, ROWS, LANES), F32),
            pltpu.VMEM((ROWS + 16, LANES), F32),
        ],
        name="second_sweep",
        **PARAMS,
    )(cf, ids, mean_field, *edges[1:], *mids, *lefts)
    return (smoothed, residual)


def solution(mesh):
    return jax.shard_map(
        body,
        mesh=mesh,
        in_specs=(
            P("mode", "space", None, None),
            P("mode", "space", None, None),
            P("space", None, None),
            P(None, "space", None, None),
            P(),
            P(),
        ),
        out_specs=(P("mode", "space", None, None), P("mode", "space", None, None)),
        check_vma=False,
    )
```

```python
import functools

import jax
import jax.numpy as jnp
from jax import lax
from jax.experimental import pallas as pl
from jax.experimental.pallas import tpu as pltpu
from jax.sharding import PartitionSpec as P

LOCAL, ROWS, LANES, HELD = 9, 64, 128, 16
GROUPS = 4
SLOTS = LOCAL * GROUPS
FIELDS = 5
ENTRIES = 156
EDGE = 18 * SLOTS
EDGE_FIELDS = ROWS + 18 * (FIELDS - 1)
UNROLL = 2
NEAR = 2 * LOCAL
F32 = jnp.float32
VMEM = pl.BlockSpec(memory_space=pltpu.VMEM)
SMEM = pl.BlockSpec(memory_space=pltpu.SMEM)
HBM = pl.BlockSpec(memory_space=pltpu.HBM)
COST = pl.CostEstimate(flops=20_000_000, bytes_accessed=12_000_000, transcendentals=0)
PARAMS = dict(compiler_params=pltpu.CompilerParams(vmem_limit_bytes=40 * 2**20))


def shape(*dims):
    return jax.ShapeDtypeStruct(dims, F32)


def window(ref, lead, g, low, count):
    rows = ref[(*lead, pl.ds(pl.multiple_of(HELD * g, HELD), 32), slice(None))]
    return rows[..., 8 + low : 8 + low + count, :]


def fill_padded(src, padded, sem):
    copy = pltpu.make_async_copy(src, padded.at[..., pl.ds(8, ROWS), :], sem)
    copy.start()
    edge = jnp.zeros((*padded.shape[:-2], 8, LANES), F32)
    padded[..., 0:8, :] = edge
    padded[..., 8 + ROWS : 16 + ROWS, :] = edge
    return copy


def lane_next(x):
    lane = lax.broadcasted_iota(jnp.int32, x.shape, x.ndim - 1)
    return jnp.where(lane == LANES - 1, 0.0, pltpu.roll(x, LANES - 1, x.ndim - 1))


def lane_prev(x):
    lane = lax.broadcasted_iota(jnp.int32, x.shape, x.ndim - 1)
    return jnp.where(lane == 0, 0.0, pltpu.roll(x, 1, x.ndim - 1))


def pack_start(ids, start, o0, o1, o2, o3):
    g = ids[0]
    for d, out in enumerate((o0, o1, o2, o3)):
        q = g ^ d
        before = pl.ds(pl.multiple_of(jnp.maximum(HELD * q - 8, 0), 8), 8)
        here = pl.ds(pl.multiple_of(HELD * q, HELD), HELD)
        after = pl.ds(pl.multiple_of(jnp.minimum(HELD * q + HELD, ROWS - 8), 8), 8)
        for k in range(LOCAL):
            for p in range(2):
                rows = [start[k, p, at, :] for at in (before, here, after)]
                at = k * 40 + 20 * p
                out[at : at + 20, :] = jnp.concatenate(rows, axis=0)[6:26]

        def clear(first):
            for k in range(LOCAL):
                for p in range(2):
                    at = k * 40 + 20 * p + first
                    out[at : at + 2, :] = jnp.zeros((2, LANES), F32)

        pl.when(q == 0)(functools.partial(clear, 0))
        pl.when(q == GROUPS - 1)(functools.partial(clear, 18))


def pack_fields(ids, mean, kl, even, odd, klp, sems):
    g, parity = ids[0], ids[1]
    two = fill_padded(kl, klp, sems.at[0])
    edges = []
    for out, plane, sem in ((even, 1 - parity, 1), (odd, parity, 2)):
        edges.append(
            pltpu.make_async_copy(mean.at[plane], out.at[pl.ds(0, ROWS), :], sems.at[sem])
        )
        edges[-1].start()
    two.wait()
    for out, plane in ((even, 1 - parity), (odd, parity)):
        for m in range(FIELDS - 1):
            at = ROWS + 18 * m
            out[at : at + 18, :] = window(klp, (m, plane), g, -1, 18)
    for edge in edges:
        edge.wait()


def pack_source(ids, source, o0, o1, o2, o3, padded, sem):
    g = ids[0]
    fill_padded(source, padded, sem).wait()
    for d, out in enumerate((o0, o1, o2, o3)):
        for p in range(2):
            for k in range(LOCAL):
                at = k * 36 + 18 * p
                out[at : at + 18, :] = window(padded, (k, p), g ^ d, -1, 18)


def edge(src, k, top, upward):
    low = src[k * 40 + 1 : k * 40 + 19, :]
    high = src[k * 40 + 21 : k * 40 + 39, :]
    return jnp.where(top == upward, high, low)


def pack_near(ids, s0, s1, odd):
    top = ids[1] == 0
    for d, src in enumerate((s0, s1)):
        for k in range(LOCAL):
            at = 18 * (LOCAL * d + k)
            odd[at : at + 18, :] = edge(src, k, top, False)


def pack_far(ids, s0, s1, s2, s3, field_even, field_odd, even, odd):
    top = ids[1] == 0
    for d, src in enumerate((s0, s1, s2, s3)):
        for k in range(LOCAL):
            pos = LOCAL * d + k
            even[18 * pos : 18 * pos + 18, :] = edge(src, k, top, True)
            if pos >= NEAR:
                at = 18 * (pos - NEAR)
                odd[at : at + 18, :] = edge(src, k, top, False)
    even[EDGE:, :] = field_even[...]
    odd[EDGE // 2 :, :] = field_odd[...]


def sides(ids, from_even, from_odd):
    top = ids[1] == 0
    return jnp.where(top, from_odd, from_even), jnp.where(top, from_even, from_odd)


def near_odd(ids, straight, relayed):
    return jnp.where(ids[2] == 1, relayed, straight)


def accumulate(trip, coef, accs, term, visit=None):
    def step(e, carry):
        for lane, acc in enumerate(accs):
            n = e * len(accs) + lane
            m, i, j, c = trip[n], trip[ENTRIES + n], trip[2 * ENTRIES + n], coef[n]
            if visit is not None:
                visit(m, i, c)
            for p in range(2):
                acc[i, p] += c * term(m, j, p)
        return carry

    lax.fori_loop(0, ENTRIES // len(accs), step, 0, unroll=UNROLL)


def first_inner(
    trip, coef, ids, s0, s1, s2, s3, mean, kl, acc, faces, inverse, klp, ae, vv, nxt, prv, diag, sems
):
    g = ids[0]
    one = fill_padded(mean, klp.at[0], sems.at[0])
    two = fill_padded(kl, klp.at[pl.ds(1, FIELDS - 1)], sems.at[1])
    for d, src in enumerate((s0, s1, s2, s3)):
        for k in range(LOCAL):
            pos = LOCAL * d + k
            for p in range(2):
                vv[pos, p, 7:27, :] = src[k * 40 + 20 * p : k * 40 + 20 * p + 20, :]
                mine = vv[pos, p, 8:32, :]
                nxt[pos, p] = lane_next(mine)
                prv[pos, p] = lane_prev(mine)
    one.wait()
    two.wait()
    for m in range(FIELDS):
        for p in range(2):
            ae[m, p, 7:27, :] = window(klp, (m, p), g, -2, 20)
    for m in range(FIELDS):
        for p in range(2):
            own = ae[m, p, 8:32, :]
            others = (
                ae[m, 1 - p, 8:32, :],
                ae[m, p, 9:33, :], ae[m, p, 7:31, :],
                lane_next(own), lane_prev(own),
            )
            total = None
            for b, other in enumerate(others):
                face = 0.5 * (own + other)
                total = face if total is None else total + face
                faces[m, 2 + b, p] = -face
            faces[m, 0, p] = total
            faces[m, 1, p] = own
    acc[...] = jnp.zeros(acc.shape, F32)

    def term(m, j, p):
        total = faces[m, 0, p] * vv[j, p, 8:32, :] + faces[m, 2, p] * vv[j, 1 - p, 8:32, :]
        total += faces[m, 3, p] * vv[j, p, 9:33, :] + faces[m, 4, p] * vv[j, p, 7:31, :]
        return total + (faces[m, 5, p] * nxt[j, p] + faces[m, 6, p] * prv[j, p])

    def visit(m, i, c):
        diag[jnp.where(m == 0, i, SLOTS)] = c

    accumulate(trip, coef, (acc,), term, visit)
    for pos in range(SLOTS):
        inverse[pos : pos + 1, :] = 1.0 / jnp.full((1, LANES), diag[pos], F32)


def first_outer(
    trip, coef, ids, inner, faces, inverse, *rest
):
    relayed, *rest = rest
    s0, s1, s2, s3, t0, t1, t2, t3, near, far, ev = rest[:11]
    mid, b0, b1, b2, b3, even, odd_a, odd_b, outer, acc, more, zz, pad = rest[11:]
    g, top = ids[0], ids[1] == 0
    for m in range(FIELDS):
        at = ROWS + 18 * (m - 1)
        rows = slice(at, at + 18) if m else slice(0, ROWS)
        e = ev[EDGE + rows.start : EDGE + rows.stop, :]
        o = far[EDGE // 2 + rows.start : EDGE // 2 + rows.stop, :]
        for p, other in enumerate(sides(ids, e, o)):
            if m == 0:
                pad[0:8, :] = jnp.zeros((8, LANES), F32)
                pad[8 : 8 + ROWS, :] = other
                pad[8 + ROWS :, :] = jnp.zeros((8, LANES), F32)
                other = window(pad, (), g, -1, 18)
            outer[m, p, 0:18, :] = 0.5 * (faces[m, 1, p, 0:18, :] + other)
    for d, src in enumerate((s0, s1, s2, s3)):
        for k in range(LOCAL):
            pos = LOCAL * d + k
            rows = slice(18 * pos, 18 * pos + 18)
            if pos < NEAR:
                o = near_odd(ids, near[rows, :], relayed[rows, :])
            else:
                o = far[18 * (pos - NEAR) : 18 * (pos - NEAR) + 18, :]
            for p, z in enumerate(sides(ids, ev[rows, :], o)):
                at = k * 40 + 20 * p + 1
                zz[pos, p, 0:18, :] = src[at : at + 18, :] - z
    acc[...] = inner[...]
    more[...] = jnp.zeros(more.shape, F32)
    accumulate(trip, coef, (acc, more), lambda m, j, p: outer[m, p] * zz[j, p])
    row = HELD * g - 1 + lax.broadcasted_iota(jnp.int32, (18, LANES), 0)
    inside = (row >= 0) & (row < ROWS)
    rates = [0.8 / (faces[0, 0, p, 0:18, :] + outer[0, p, 0:18, :]) for p in range(2)]
    for d, (start, src, out) in enumerate(
        ((s0, t0, b0), (s1, t1, b1), (s2, t2, b2), (s3, t3, b3))
    ):
        for k in range(LOCAL):
            pos = LOCAL * d + k
            helds = []
            for p in range(2):
                at = k * 36 + 18 * p
                first = src[at : at + 18, :] - (acc[pos, p, 0:18, :] + more[pos, p, 0:18, :])
                at = k * 40 + 20 * p + 1
                moved = start[at : at + 18, :] + first * rates[p] * inverse[pos : pos + 1, :]
                moved = jnp.where(inside, moved, 0.0)
                mid[pos, p, 7:25, :] = moved
                held = moved[1 : 1 + HELD]
                out[k, p] = held
                helds.append(held)
            even[pos] = jnp.where(top, helds[1], helds[0])
            (odd_a if pos < NEAR else odd_b)[pos % NEAR] = jnp.where(top, helds[0], helds[1])


def second_inner(trip, coef, ids, mid, faces, acc, nxt, prv):
    for pos in range(SLOTS):
        for p in range(2):
            mine = mid[pos, p, 8:24, :]
            nxt[pos, p] = lane_next(mine)
            prv[pos, p] = lane_prev(mine)
    acc[...] = jnp.zeros(acc.shape, F32)
    held = slice(1, 1 + HELD)

    def term(m, j, p):
        total = faces[m, 0, p, held] * mid[j, p, 8:24, :]
        total += faces[m, 2, p, held] * mid[j, 1 - p, 8:24, :]
        total += faces[m, 3, p, held] * mid[j, p, 9:25, :] + faces[m, 4, p, held] * mid[j, p, 7:23, :]
        return total + (faces[m, 5, p, held] * nxt[j, p] + faces[m, 6, p, held] * prv[j, p])

    accumulate(trip, coef, (acc,), term)


def second_outer(trip, coef, ids, inner, outer, mid, *rest):
    relayed, *rest = rest
    t0, t1, t2, t3, near, far, ev, o0, o1, o2, o3, acc, more, zz = rest
    for pos in range(SLOTS):
        if pos < NEAR:
            o = near_odd(ids, near[pos], relayed[pos])
        else:
            o = far[pos - NEAR]
        for p, z in enumerate(sides(ids, ev[pos], o)):
            zz[pos, p] = mid[pos, p, 8:24, :] - z
    acc[...] = inner[...]
    more[...] = jnp.zeros(more.shape, F32)
    held = slice(1, 1 + HELD)
    accumulate(trip, coef, (acc, more), lambda m, j, p: outer[m, p, held] * zz[j, p])
    for d, (src, out) in enumerate(((t0, o0), (t1, o1), (t2, o2), (t3, o3))):
        for k in range(LOCAL):
            for p in range(2):
                at = k * 36 + 18 * p + 1
                pos = LOCAL * d + k
                out[k, p] = src[at : at + HELD, :] - (acc[pos, p] + more[pos, p])


def final_rates(ids, mean, far, ev, rate, pad):
    below, above = sides(ids, ev[EDGE : EDGE + ROWS, :], far[EDGE // 2 : EDGE // 2 + ROWS, :])
    pad[0:8, :] = jnp.zeros((8, LANES), F32)
    pad[8 + ROWS :, :] = jnp.zeros((8, LANES), F32)
    for p in range(2):
        own = mean[p]
        pad[8 : 8 + ROWS, :] = own
        others = (
            above if p else mean[1], mean[0] if p else below,
            pad[9 : 9 + ROWS, :], pad[7 : 7 + ROWS, :],
            lane_next(own), lane_prev(own),
        )
        total = None
        for other in others:
            face = 0.5 * (own + other)
            total = face if total is None else total + face
        rate[p] = 0.8 / total


def second_sweep(ids, rate, inverse, m0, m1, m2, m3, r0, r1, r2, r3, smoothed, residual):
    g = ids[0]
    for d, (mid, res) in enumerate(((m0, r0), (m1, r1), (m2, r2), (m3, r3))):
        rows = pl.ds(pl.multiple_of(HELD * (g ^ d), HELD), HELD)
        for p in range(2):
            here = rate[p, rows, :]
            for k in range(LOCAL):
                left = res[k, p]
                residual[k, p, rows, :] = left
                smoothed[k, p, rows, :] = mid[k, p] + left * here * inverse[k : k + 1, :]


def body(start_field, source, mean_field, kl_fields, triples, coef):
    g = lax.axis_index("mode").astype(jnp.int32)
    slab = lax.axis_index("space").astype(jnp.int32)
    ids = jnp.stack([g, slab % 2, ((slab % 4 == 0) | (slab % 4 == 3)).astype(jnp.int32)])
    count = lax.axis_size("space")
    def both(pairs):
        return [pair for a, b in pairs for pair in ((a, b), (b, a))]

    evens = both([(i, i + 1) for i in range(0, count, 2)])
    odds = both([(i, i + 1) for i in range(1, count - 1, 2)])
    inner = [(i + 1, i + 2) for i in range(0, count, 4)]
    hops = both(inner + [(i, i + 3) for i in range(0, count, 4)])
    relay = [(i, i + 4) for i in range(0, count - 4, 4)]
    relay += [(i + 7, i + 3) for i in range(0, count - 4, 4)]

    def meet(x, pairs):
        return lax.ppermute(x, "space", pairs)

    def trade(parts):
        return [parts[0]] + [
            lax.ppermute(parts[d], "mode", [(i, i ^ d) for i in range(GROUPS)])
            for d in range(1, GROUPS)
        ]

    sends = pl.pallas_call(
        pack_start,
        out_shape=[shape(360, LANES)] * 4,
        in_specs=[SMEM, VMEM],
        out_specs=[VMEM] * 4,
        name="pack_start",
        **PARAMS,
    )(ids, start_field)
    starts = trade(sends)
    near = pl.pallas_call(
        pack_near,
        out_shape=shape(EDGE // 2, LANES),
        in_specs=[SMEM] + [VMEM] * 2,
        out_specs=VMEM,
        name="pack_near",
        **PARAMS,
    )(ids, *starts[:2])
    mean_late, kl_late, source, near = lax.optimization_barrier(
        (mean_field, kl_fields, source, near)
    )
    near = meet(near, hops)
    *parts, starts[3] = lax.optimization_barrier((
        *pl.pallas_call(
            pack_source,
            out_shape=[shape(324, LANES)] * 4,
            in_specs=[SMEM, HBM],
            out_specs=[VMEM] * 4,
            scratch_shapes=[
                pltpu.VMEM((LOCAL, 2, ROWS + 16, LANES), F32), pltpu.SemaphoreType.DMA
            ],
            name="pack_source",
            **PARAMS,
        )(ids, source),
        starts[3],
    ))
    sources = trade(parts)
    triples, starts[2], sources[1], near = lax.optimization_barrier(
        (triples, starts[2], sources[1], near)
    )
    modes = triples[:, 1:]
    at = LOCAL * ((modes // LOCAL) ^ g) + modes % LOCAL
    trip = jnp.concatenate([triples[:, 0], at[:, 0], at[:, 1]])
    fields = pl.pallas_call(
        pack_fields,
        out_shape=[shape(EDGE_FIELDS, LANES)] * 2,
        in_specs=[SMEM, HBM, HBM],
        out_specs=[VMEM] * 2,
        scratch_shapes=[
            pltpu.VMEM((FIELDS - 1, 2, ROWS + 16, LANES), F32),
            pltpu.SemaphoreType.DMA((3,)),
        ],
        name="pack_fields",
        **PARAMS,
    )(ids, mean_late, kl_late)
    even, odd = pl.pallas_call(
        pack_far,
        out_shape=[shape(EDGE + EDGE_FIELDS, LANES), shape(EDGE // 2 + EDGE_FIELDS, LANES)],
        in_specs=[SMEM] + [VMEM] * 6,
        out_specs=[VMEM] * 2,
        name="pack_far",
        **PARAMS,
    )(ids, *starts, *fields)
    edges = (near, meet(odd, odds), meet(even, evens))
    relayed = meet(near, relay)
    acc, faces, inverse = pl.pallas_call(
        first_inner,
        out_shape=[
            shape(SLOTS, 2, 24, LANES), shape(FIELDS, 7, 2, 24, LANES), shape(SLOTS, LANES)
        ],
        in_specs=[SMEM] * 3 + [VMEM] * 4 + [HBM] * 2,
        out_specs=[VMEM] * 3,
        scratch_shapes=[
            pltpu.VMEM((FIELDS, 2, ROWS + 16, LANES), F32),
            pltpu.VMEM((FIELDS, 2, 40, LANES), F32),
            pltpu.VMEM((SLOTS, 2, 40, LANES), F32),
            pltpu.VMEM((SLOTS, 2, 24, LANES), F32),
            pltpu.VMEM((SLOTS, 2, 24, LANES), F32),
            pltpu.SMEM((SLOTS + 1,), F32),
            pltpu.SemaphoreType.DMA((2,)),
        ],
        cost_estimate=COST,
        name="first_inner",
        **PARAMS,
    )(trip, coef, ids, *starts, mean_field, kl_fields)
    operands = (trip, coef, ids, acc, faces, inverse, relayed, *starts, *sources, *edges)
    mid, *mids, even, odd_a, odd_b, outer = pl.pallas_call(
        first_outer,
        out_shape=[shape(SLOTS, 2, 32, LANES)]
        + [shape(LOCAL, 2, HELD, LANES)] * 4
        + [shape(SLOTS, HELD, LANES)]
        + [shape(SLOTS // 2, HELD, LANES)] * 2
        + [shape(FIELDS, 2, 24, LANES)],
        in_specs=[SMEM] * 3 + [VMEM] * (len(operands) - 3),
        out_specs=[VMEM] * 9,
        scratch_shapes=[pltpu.VMEM((SLOTS, 2, 24, LANES), F32)] * 3
        + [pltpu.VMEM((ROWS + 16, LANES), F32)],
        name="first_outer",
        **PARAMS,
    )(*operands)
    near = meet(odd_a, hops)
    met = (near, meet(odd_b, odds), meet(even, evens))
    relayed = meet(near, relay)
    mids = trade(mids)
    acc = pl.pallas_call(
        second_inner,
        out_shape=shape(SLOTS, 2, HELD, LANES),
        in_specs=[SMEM] * 3 + [VMEM] * 2,
        out_specs=VMEM,
        scratch_shapes=[pltpu.VMEM((SLOTS, 2, HELD, LANES), F32)] * 2,
        cost_estimate=COST,
        name="second_inner",
        **PARAMS,
    )(trip, coef, ids, mid, faces)
    operands = (trip, coef, ids, acc, outer, mid, relayed, *sources, *met)
    lefts = pl.pallas_call(
        second_outer,
        out_shape=[shape(LOCAL, 2, HELD, LANES)] * 4,
        in_specs=[SMEM] * 3 + [VMEM] * (len(operands) - 3),
        out_specs=[VMEM] * 4,
        scratch_shapes=[pltpu.VMEM((SLOTS, 2, HELD, LANES), F32)] * 3,
        name="second_outer",
        **PARAMS,
    )(*operands)
    lefts = trade(lefts)
    rate = pl.pallas_call(
        final_rates,
        out_shape=shape(2, ROWS, LANES),
        in_specs=[SMEM] + [VMEM] * 3,
        out_specs=VMEM,
        scratch_shapes=[pltpu.VMEM((ROWS + 16, LANES), F32)],
        name="final_rates",
        **PARAMS,
    )(ids, mean_field, *edges[1:])
    smoothed, residual = pl.pallas_call(
        second_sweep,
        out_shape=[shape(LOCAL, 2, ROWS, LANES)] * 2,
        in_specs=[SMEM] + [VMEM] * 10,
        out_specs=[VMEM] * 2,
        name="second_sweep",
        **PARAMS,
    )(ids, rate, inverse, *mids, *lefts)
    return (smoothed, residual)


def solution(mesh):
    return jax.shard_map(
        body,
        mesh=mesh,
        in_specs=(
            P("mode", "space", None, None),
            P("mode", "space", None, None),
            P("space", None, None),
            P(None, "space", None, None),
            P(),
            P(),
        ),
        out_specs=(P("mode", "space", None, None), P("mode", "space", None, None)),
        check_vma=False,
    )
```

```python
import functools

import jax
import jax.numpy as jnp
from jax import lax
from jax.experimental import pallas as pl
from jax.experimental.pallas import tpu as pltpu
from jax.sharding import PartitionSpec as P

LOCAL, ROWS, LANES, HELD = 9, 64, 128, 16
GROUPS = 4
SLOTS = LOCAL * GROUPS
FIELDS = 5
ENTRIES = 156
EDGE = 18 * SLOTS
EDGE_FIELDS = ROWS + 18 * (FIELDS - 1)
UNROLL = 3
NEAR = 2 * LOCAL
F32 = jnp.float32
VMEM = pl.BlockSpec(memory_space=pltpu.VMEM)
SMEM = pl.BlockSpec(memory_space=pltpu.SMEM)
HBM = pl.BlockSpec(memory_space=pltpu.HBM)
COST = pl.CostEstimate(flops=20_000_000, bytes_accessed=12_000_000, transcendentals=0)
SIDE_COST = pl.CostEstimate(flops=5_000_000, bytes_accessed=3_000_000, transcendentals=0)
PARAMS = dict(compiler_params=pltpu.CompilerParams(vmem_limit_bytes=40 * 2**20))


def shape(*dims):
    return jax.ShapeDtypeStruct(dims, F32)


def window(ref, lead, g, low, count):
    rows = ref[(*lead, pl.ds(pl.multiple_of(HELD * g, HELD), 32), slice(None))]
    return rows[..., 8 + low : 8 + low + count, :]


def fill_padded(src, padded, sem):
    copy = pltpu.make_async_copy(src, padded.at[..., pl.ds(8, ROWS), :], sem)
    copy.start()
    edge = jnp.zeros((*padded.shape[:-2], 8, LANES), F32)
    padded[..., 0:8, :] = edge
    padded[..., 8 + ROWS : 16 + ROWS, :] = edge
    return copy


def lane_next(x):
    lane = lax.broadcasted_iota(jnp.int32, x.shape, x.ndim - 1)
    return jnp.where(lane == LANES - 1, 0.0, pltpu.roll(x, LANES - 1, x.ndim - 1))


def lane_prev(x):
    lane = lax.broadcasted_iota(jnp.int32, x.shape, x.ndim - 1)
    return jnp.where(lane == 0, 0.0, pltpu.roll(x, 1, x.ndim - 1))


def pack_start(ids, start, o0, o1, o2, o3):
    g = ids[0]
    for d, out in enumerate((o0, o1, o2, o3)):
        q = g ^ d
        before = pl.ds(pl.multiple_of(jnp.maximum(HELD * q - 8, 0), 8), 8)
        here = pl.ds(pl.multiple_of(HELD * q, HELD), HELD)
        after = pl.ds(pl.multiple_of(jnp.minimum(HELD * q + HELD, ROWS - 8), 8), 8)
        for k in range(LOCAL):
            for p in range(2):
                rows = [start[k, p, at, :] for at in (before, here, after)]
                at = k * 40 + 20 * p
                out[at : at + 20, :] = jnp.concatenate(rows, axis=0)[6:26]

        def clear(first):
            for k in range(LOCAL):
                for p in range(2):
                    at = k * 40 + 20 * p + first
                    out[at : at + 2, :] = jnp.zeros((2, LANES), F32)

        pl.when(q == 0)(functools.partial(clear, 0))
        pl.when(q == GROUPS - 1)(functools.partial(clear, 18))


def pack_fields(ids, mean, kl, even, odd, own, padded, sems):
    g, parity = ids[0], ids[1]
    one = fill_padded(mean, padded.at[0], sems.at[0])
    two = fill_padded(kl, padded.at[pl.ds(1, FIELDS - 1)], sems.at[1])
    one.wait()
    two.wait()
    for m in range(FIELDS):
        for p in range(2):
            own[m, p, 7:27, :] = window(padded, (m, p), g, -2, 20)
    for out, plane in ((even, 1 - parity), (odd, parity)):
        out[0:ROWS, :] = padded[0, plane, 8 : 8 + ROWS, :]
        for m in range(1, FIELDS):
            at = ROWS + 18 * (m - 1)
            out[at : at + 18, :] = own[m, plane, 8:26, :]


def pack_source(ids, source, o0, o1, o2, o3, padded, sem):
    g = ids[0]
    fill_padded(source, padded, sem).wait()
    for d, out in enumerate((o0, o1, o2, o3)):
        for p in range(2):
            for k in range(LOCAL):
                at = k * 36 + 18 * p
                out[at : at + 18, :] = window(padded, (k, p), g ^ d, -1, 18)


def edge(src, k, top, upward):
    low = src[k * 40 + 1 : k * 40 + 19, :]
    high = src[k * 40 + 21 : k * 40 + 39, :]
    return jnp.where(top == upward, high, low)


def pack_near(ids, s0, s1, odd):
    top = ids[1] == 0
    for d, src in enumerate((s0, s1)):
        for k in range(LOCAL):
            at = 18 * (LOCAL * d + k)
            odd[at : at + 18, :] = edge(src, k, top, False)


def pack_far(ids, s0, s1, s2, s3, field_even, field_odd, even, odd):
    top = ids[1] == 0
    for d, src in enumerate((s0, s1, s2, s3)):
        for k in range(LOCAL):
            pos = LOCAL * d + k
            even[18 * pos : 18 * pos + 18, :] = edge(src, k, top, True)
            if pos >= NEAR:
                at = 18 * (pos - NEAR)
                odd[at : at + 18, :] = edge(src, k, top, False)
    even[EDGE:, :] = field_even[...]
    odd[EDGE // 2 :, :] = field_odd[...]


def sides(ids, from_even, from_odd):
    top = ids[1] == 0
    return jnp.where(top, from_odd, from_even), jnp.where(top, from_even, from_odd)


def near_odd(ids, straight, relayed):
    return jnp.where(ids[2] == 1, relayed, straight)


def rows_of(src, plane, lower, upper, count):
    low, high = src[lower : lower + count, :], src[upper : upper + count, :]
    return jnp.where(plane == 0, low, high)


def accumulate(trip, coef, accs, term, visit=None):
    def step(e, carry):
        for lane, acc in enumerate(accs):
            n = e * len(accs) + lane
            m, i, j, c = trip[n], trip[ENTRIES + n], trip[2 * ENTRIES + n], coef[n]
            if visit is not None:
                visit(m, i, c)
            term(acc, m, i, j, c)
        return carry

    lax.fori_loop(0, ENTRIES // len(accs), step, 0, unroll=UNROLL)


def first_inner(
    trip, coef, s0, s1, s2, s3, ae, acc, faces, inverse, vv, nxt, prv, diag
):
    for d, src in enumerate((s0, s1, s2, s3)):
        for k in range(LOCAL):
            pos = LOCAL * d + k
            for p in range(2):
                vv[pos, p, 7:27, :] = src[k * 40 + 20 * p : k * 40 + 20 * p + 20, :]
                mine = vv[pos, p, 8:32, :]
                nxt[pos, p] = lane_next(mine)
                prv[pos, p] = lane_prev(mine)
    for m in range(FIELDS):
        for p in range(2):
            own = ae[m, p, 8:32, :]
            others = (
                ae[m, 1 - p, 8:32, :],
                ae[m, p, 9:33, :], ae[m, p, 7:31, :],
                lane_next(own), lane_prev(own),
            )
            total = None
            for b, other in enumerate(others):
                face = 0.5 * (own + other)
                total = face if total is None else total + face
                faces[m, 2 + b, p] = -face
            faces[m, 0, p] = total
            faces[m, 1, p] = own
    acc[...] = jnp.zeros(acc.shape, F32)

    def term(acc, m, i, j, c):
        for p in range(2):
            total = faces[m, 0, p] * vv[j, p, 8:32, :] + faces[m, 2, p] * vv[j, 1 - p, 8:32, :]
            total += faces[m, 3, p] * vv[j, p, 9:33, :] + faces[m, 4, p] * vv[j, p, 7:31, :]
            total += faces[m, 5, p] * nxt[j, p] + faces[m, 6, p] * prv[j, p]
            acc[i, p] += c * total

    def visit(m, i, c):
        diag[jnp.where(m == 0, i, SLOTS)] = c

    accumulate(trip, coef, (acc,), term, visit)
    for pos in range(SLOTS):
        inverse[pos : pos + 1, :] = 1.0 / jnp.full((1, LANES), diag[pos], F32)


def first_side(odd, trip, coef, ids, inner, faces, inverse, *rest):
    count = 3 if odd else 1
    planes, rest = rest[:count], rest[count:]
    starts, sources, rest = rest[:4], rest[4:8], rest[8:]
    mid, *sends, outer, acc, more, zz, pad = rest
    g = ids[0]
    p = ids[1] if odd else 1 - ids[1]
    if odd:
        near, far, relayed = planes
        base, fields = EDGE // 2, far
    else:
        base, fields = EDGE, planes[0]
    for m in range(FIELDS):
        at = base + ROWS + 18 * (m - 1)
        if m == 0:
            pad[0:8, :] = jnp.zeros((8, LANES), F32)
            pad[8 : 8 + ROWS, :] = fields[base : base + ROWS, :]
            pad[8 + ROWS :, :] = jnp.zeros((8, LANES), F32)
            other = window(pad, (), g, -1, 18)
        else:
            other = fields[at : at + 18, :]
        outer[m, 0:18, :] = 0.5 * (faces[m, 1, p, 0:18, :] + other)
    for pos in range(SLOTS):
        rows = slice(18 * pos, 18 * pos + 18)
        if not odd:
            z = planes[0][rows, :]
        elif pos < NEAR:
            z = near_odd(ids, near[rows, :], relayed[rows, :])
        else:
            z = far[18 * (pos - NEAR) : 18 * (pos - NEAR) + 18, :]
        at = pos % LOCAL * 40 + 1
        zz[pos, 0:18, :] = rows_of(starts[pos // LOCAL], p, at, at + 20, 18) - z
    acc[...] = inner[:, p]
    more[...] = jnp.zeros(more.shape, F32)

    def term(acc, m, i, j, c):
        acc[i] += c * (outer[m] * zz[j])

    accumulate(trip, coef, (acc, more), term)
    row = HELD * g - 1 + lax.broadcasted_iota(jnp.int32, (18, LANES), 0)
    inside = (row >= 0) & (row < ROWS)
    rate = 0.8 / (faces[0, 0, p, 0:18, :] + outer[0, 0:18, :])
    for pos in range(SLOTS):
        at = pos % LOCAL * 36
        first = rows_of(sources[pos // LOCAL], p, at, at + 18, 18)
        first = first - (acc[pos, 0:18, :] + more[pos, 0:18, :])
        at = pos % LOCAL * 40 + 1
        moved = rows_of(starts[pos // LOCAL], p, at, at + 20, 18)
        moved = moved + first * rate * inverse[pos : pos + 1, :]
        moved = jnp.where(inside, moved, 0.0)
        mid[pos, 7:25, :] = moved
        if odd:
            sends[pos // NEAR][pos % NEAR] = moved[1 : 1 + HELD]
        else:
            sends[0][pos] = moved[1 : 1 + HELD]


HERE = slice(1, 1 + HELD)


def in_plane(faces, p, m, j, mine, other, nxt, prv):
    total = faces[m, 0, p, HERE] * mine[j, 8:24, :] + faces[m, 2, p, HERE] * other[j, 8:24, :]
    total += faces[m, 3, p, HERE] * mine[j, 9:25, :] + faces[m, 4, p, HERE] * mine[j, 7:23, :]
    return total + (faces[m, 5, p, HERE] * nxt[j] + faces[m, 6, p, HERE] * prv[j])


def shift_lanes(mine, nxt, prv):
    for pos in range(SLOTS):
        held = mine[pos, 8:24, :]
        nxt[pos] = lane_next(held)
        prv[pos] = lane_prev(held)


def second_even(
    trip, coef, ids, faces, outer, mine, other, met, t0, t1, t2, t3, o0, o1, o2, o3,
    acc, more, zz, nxt, prv,
):
    p = 1 - ids[1]
    shift_lanes(mine, nxt, prv)
    for pos in range(SLOTS):
        zz[pos] = mine[pos, 8:24, :] - met[pos]
    acc[...] = jnp.zeros(acc.shape, F32)
    more[...] = jnp.zeros(more.shape, F32)

    def term(acc, m, i, j, c):
        total = in_plane(faces, p, m, j, mine, other, nxt, prv)
        acc[i] += c * (total + outer[m, HERE] * zz[j])

    accumulate(trip, coef, (acc, more), term)
    for d, (src, out) in enumerate(((t0, o0), (t1, o1), (t2, o2), (t3, o3))):
        for k in range(LOCAL):
            pos = LOCAL * d + k
            out[k, 0] = mine[pos, 8:24, :]
            out[k, 1] = other[pos, 8:24, :]
            at = k * 36 + 1
            out[k, 2] = rows_of(src, p, at, at + 18, HELD) - (acc[pos] + more[pos])


def second_inner(trip, coef, ids, faces, mine, other, acc, more, nxt, prv):
    p = ids[1]
    shift_lanes(mine, nxt, prv)
    acc[...] = jnp.zeros(acc.shape, F32)
    more[...] = jnp.zeros(more.shape, F32)

    def term(acc, m, i, j, c):
        acc[i] += c * in_plane(faces, p, m, j, mine, other, nxt, prv)

    accumulate(trip, coef, (acc, more), term)


def second_odd(
    trip, coef, ids, inner, extra, outer, mine, near, far, relayed, t0, t1, t2, t3,
    o0, o1, o2, o3, acc, more, zz,
):
    p = ids[1]
    for pos in range(SLOTS):
        z = near_odd(ids, near[pos], relayed[pos]) if pos < NEAR else far[pos - NEAR]
        zz[pos] = mine[pos, 8:24, :] - z
    acc[...] = inner[...]
    more[...] = extra[...]

    def term(acc, m, i, j, c):
        acc[i] += c * (outer[m, HERE] * zz[j])

    accumulate(trip, coef, (acc, more), term)
    for d, (src, out) in enumerate(((t0, o0), (t1, o1), (t2, o2), (t3, o3))):
        for k in range(LOCAL):
            pos = LOCAL * d + k
            at = k * 36 + 1
            out[k] = rows_of(src, p, at, at + 18, HELD) - (acc[pos] + more[pos])


def final_rates(ids, mean, far, ev, rate, pad):
    below, above = sides(ids, ev[EDGE : EDGE + ROWS, :], far[EDGE // 2 : EDGE // 2 + ROWS, :])
    pad[0:8, :] = jnp.zeros((8, LANES), F32)
    pad[8 + ROWS :, :] = jnp.zeros((8, LANES), F32)
    for p in range(2):
        own = mean[p]
        pad[8 : 8 + ROWS, :] = own
        others = (
            above if p else mean[1], mean[0] if p else below,
            pad[9 : 9 + ROWS, :], pad[7 : 7 + ROWS, :],
            lane_next(own), lane_prev(own),
        )
        total = None
        for other in others:
            face = 0.5 * (own + other)
            total = face if total is None else total + face
        rate[p] = 0.8 / total


def second_sweep(ids, rate, inverse, m0, m1, m2, m3, r0, r1, r2, r3, smoothed, residual):
    g, parity = ids[0], ids[1]
    for d, (mid, res) in enumerate(((m0, r0), (m1, r1), (m2, r2), (m3, r3))):
        rows = pl.ds(pl.multiple_of(HELD * (g ^ d), HELD), HELD)
        for p in (0, 1):
            plane = parity if p else 1 - parity
            here = rate[plane, rows, :]
            for k in range(LOCAL):
                left = res[k] if p else mid[k, 2]
                residual[k, plane, rows, :] = left
                smoothed[k, plane, rows, :] = mid[k, p] + left * here * inverse[k : k + 1, :]


def body(start_field, source, mean_field, kl_fields, triples, coef):
    g = lax.axis_index("mode").astype(jnp.int32)
    slab = lax.axis_index("space").astype(jnp.int32)
    ids = jnp.stack([g, slab % 2, ((slab % 4 == 0) | (slab % 4 == 3)).astype(jnp.int32)])
    count = lax.axis_size("space")
    def both(pairs):
        return [pair for a, b in pairs for pair in ((a, b), (b, a))]

    evens = both([(i, i + 1) for i in range(0, count, 2)])
    odds = both([(i, i + 1) for i in range(1, count - 1, 2)])
    inner = [(i + 1, i + 2) for i in range(0, count, 4)]
    hops = both(inner + [(i, i + 3) for i in range(0, count, 4)])
    relay = [(i, i + 4) for i in range(0, count - 4, 4)]
    relay += [(i + 7, i + 3) for i in range(0, count - 4, 4)]

    def meet(x, pairs):
        return lax.ppermute(x, "space", pairs)

    def trade(parts):
        return [parts[0]] + [
            lax.ppermute(parts[d], "mode", [(i, i ^ d) for i in range(GROUPS)])
            for d in range(1, GROUPS)
        ]

    sends = pl.pallas_call(
        pack_start,
        out_shape=[shape(360, LANES)] * 4,
        in_specs=[SMEM, VMEM],
        out_specs=[VMEM] * 4,
        name="pack_start",
        **PARAMS,
    )(ids, start_field)
    starts = trade(sends)
    near = pl.pallas_call(
        pack_near,
        out_shape=shape(EDGE // 2, LANES),
        in_specs=[SMEM] + [VMEM] * 2,
        out_specs=VMEM,
        name="pack_near",
        **PARAMS,
    )(ids, *starts[:2])
    mean_late, kl_late, source, near = lax.optimization_barrier(
        (mean_field, kl_fields, source, near)
    )
    near = meet(near, hops)
    *parts, starts[3] = lax.optimization_barrier((
        *pl.pallas_call(
            pack_source,
            out_shape=[shape(324, LANES)] * 4,
            in_specs=[SMEM, HBM],
            out_specs=[VMEM] * 4,
            scratch_shapes=[
                pltpu.VMEM((LOCAL, 2, ROWS + 16, LANES), F32), pltpu.SemaphoreType.DMA
            ],
            name="pack_source",
            **PARAMS,
        )(ids, source),
        starts[3],
    ))
    sources = trade(parts)
    triples, starts[2], sources[1], near = lax.optimization_barrier(
        (triples, starts[2], sources[1], near)
    )
    modes = triples[:, 1:]
    at = LOCAL * ((modes // LOCAL) ^ g) + modes % LOCAL
    trip = jnp.concatenate([triples[:, 0], at[:, 0], at[:, 1]])
    *fields, own_fields = pl.pallas_call(
        pack_fields,
        out_shape=[shape(EDGE_FIELDS, LANES)] * 2 + [shape(FIELDS, 2, 40, LANES)],
        in_specs=[SMEM, HBM, HBM],
        out_specs=[VMEM] * 3,
        scratch_shapes=[
            pltpu.VMEM((FIELDS, 2, ROWS + 16, LANES), F32),
            pltpu.SemaphoreType.DMA((2,)),
        ],
        name="pack_fields",
        **PARAMS,
    )(ids, mean_late, kl_late)
    even, odd = pl.pallas_call(
        pack_far,
        out_shape=[shape(EDGE + EDGE_FIELDS, LANES), shape(EDGE // 2 + EDGE_FIELDS, LANES)],
        in_specs=[SMEM] + [VMEM] * 6,
        out_specs=[VMEM] * 2,
        name="pack_far",
        **PARAMS,
    )(ids, *starts, *fields)
    edges = (near, meet(odd, odds), meet(even, evens))
    relayed = meet(near, relay)
    acc, faces, inverse = pl.pallas_call(
        first_inner,
        out_shape=[
            shape(SLOTS, 2, 24, LANES), shape(FIELDS, 7, 2, 24, LANES), shape(SLOTS, LANES)
        ],
        in_specs=[SMEM] * 2 + [VMEM] * 5,
        out_specs=[VMEM] * 3,
        scratch_shapes=[
            pltpu.VMEM((SLOTS, 2, 40, LANES), F32),
            pltpu.VMEM((SLOTS, 2, 24, LANES), F32),
            pltpu.VMEM((SLOTS, 2, 24, LANES), F32),
            pltpu.SMEM((SLOTS + 1,), F32),
        ],
        cost_estimate=COST,
        name="first_inner",
        **PARAMS,
    )(trip, coef, *starts, own_fields)
    def side(odd, planes, sends):
        operands = (trip, coef, ids, acc, faces, inverse, *planes, *starts, *sources)
        return pl.pallas_call(
            functools.partial(first_side, odd),
            out_shape=[shape(SLOTS, 32, LANES)]
            + [shape(SLOTS // sends, HELD, LANES)] * sends
            + [shape(FIELDS, 24, LANES)],
            in_specs=[SMEM] * 3 + [VMEM] * (len(operands) - 3),
            out_specs=[VMEM] * (2 + sends),
            scratch_shapes=[pltpu.VMEM((SLOTS, 24, LANES), F32)] * 3
            + [pltpu.VMEM((ROWS + 16, LANES), F32)],
            cost_estimate=SIDE_COST,
            name="first_odd" if odd else "first_even",
            **PARAMS,
        )(*operands)

    near, far, even = edges
    mid_even, even, outer_even = side(False, (even,), 1)
    even = meet(even, evens)
    mid_odd, odd_a, odd_b, outer_odd = side(True, (near, far, relayed), 2)
    near = meet(odd_a, hops)
    far = meet(odd_b, odds)
    relayed = meet(near, relay)
    held = pltpu.VMEM((SLOTS, HELD, LANES), F32)
    mids = trade(pl.pallas_call(
        second_even,
        out_shape=[shape(LOCAL, 3, HELD, LANES)] * 4,
        in_specs=[SMEM] * 3 + [VMEM] * 9,
        out_specs=[VMEM] * 4,
        scratch_shapes=[held] * 5,
        cost_estimate=COST,
        name="second_even",
        **PARAMS,
    )(trip, coef, ids, faces, outer_even, mid_even, mid_odd, even, *sources))
    acc = pl.pallas_call(
        second_inner,
        out_shape=[shape(SLOTS, HELD, LANES)] * 2,
        in_specs=[SMEM] * 3 + [VMEM] * 3,
        out_specs=[VMEM] * 2,
        scratch_shapes=[held] * 2,
        cost_estimate=COST,
        name="second_inner",
        **PARAMS,
    )(trip, coef, ids, faces, mid_odd, mid_even)
    lefts = trade(pl.pallas_call(
        second_odd,
        out_shape=[shape(LOCAL, HELD, LANES)] * 4,
        in_specs=[SMEM] * 3 + [VMEM] * 11,
        out_specs=[VMEM] * 4,
        scratch_shapes=[held] * 3,
        name="second_odd",
        **PARAMS,
    )(trip, coef, ids, *acc, outer_odd, mid_odd, near, far, relayed, *sources))
    rate = pl.pallas_call(
        final_rates,
        out_shape=shape(2, ROWS, LANES),
        in_specs=[SMEM] + [VMEM] * 3,
        out_specs=VMEM,
        scratch_shapes=[pltpu.VMEM((ROWS + 16, LANES), F32)],
        name="final_rates",
        **PARAMS,
    )(ids, mean_field, *edges[1:])
    smoothed, residual = pl.pallas_call(
        second_sweep,
        out_shape=[shape(LOCAL, 2, ROWS, LANES)] * 2,
        in_specs=[SMEM] + [VMEM] * 10,
        out_specs=[VMEM] * 2,
        name="second_sweep",
        **PARAMS,
    )(ids, rate, inverse, *mids, *lefts)
    return (smoothed, residual)


def solution(mesh):
    return jax.shard_map(
        body,
        mesh=mesh,
        in_specs=(
            P("mode", "space", None, None),
            P("mode", "space", None, None),
            P("space", None, None),
            P(None, "space", None, None),
            P(),
            P(),
        ),
        out_specs=(P("mode", "space", None, None), P("mode", "space", None, None)),
        check_vma=False,
    )
```

```python
import functools

import jax
import jax.numpy as jnp
from jax import lax
from jax.experimental import pallas as pl
from jax.experimental.pallas import tpu as pltpu
from jax.sharding import PartitionSpec as P

LOCAL, ROWS, LANES, HELD = 9, 64, 128, 16
GROUPS = 4
SLOTS = LOCAL * GROUPS
FIELDS = 5
ENTRIES = 156
EDGE = 18 * SLOTS
EDGE_FIELDS = ROWS + 18 * (FIELDS - 1)
UNROLL = 6
NEAR = 2 * LOCAL
F32 = jnp.float32
VMEM = pl.BlockSpec(memory_space=pltpu.VMEM)
SMEM = pl.BlockSpec(memory_space=pltpu.SMEM)
HBM = pl.BlockSpec(memory_space=pltpu.HBM)
COST = pl.CostEstimate(flops=20_000_000, bytes_accessed=12_000_000, transcendentals=0)
SIDE_COST = pl.CostEstimate(flops=5_000_000, bytes_accessed=3_000_000, transcendentals=0)
PARAMS = dict(compiler_params=pltpu.CompilerParams(vmem_limit_bytes=40 * 2**20))


def shape(*dims):
    return jax.ShapeDtypeStruct(dims, F32)


def window(ref, lead, g, low, count):
    rows = ref[(*lead, pl.ds(pl.multiple_of(HELD * g, HELD), 32), slice(None))]
    return rows[..., 8 + low : 8 + low + count, :]


def fill_padded(src, padded, sem):
    copy = pltpu.make_async_copy(src, padded.at[..., pl.ds(8, ROWS), :], sem)
    copy.start()
    edge = jnp.zeros((*padded.shape[:-2], 8, LANES), F32)
    padded[..., 0:8, :] = edge
    padded[..., 8 + ROWS : 16 + ROWS, :] = edge
    return copy


def lane_next(x):
    lane = lax.broadcasted_iota(jnp.int32, x.shape, x.ndim - 1)
    return jnp.where(lane == LANES - 1, 0.0, pltpu.roll(x, LANES - 1, x.ndim - 1))


def lane_prev(x):
    lane = lax.broadcasted_iota(jnp.int32, x.shape, x.ndim - 1)
    return jnp.where(lane == 0, 0.0, pltpu.roll(x, 1, x.ndim - 1))


def pack_start(ids, start, o0, o1, o2, o3):
    g = ids[0]
    for d, out in enumerate((o0, o1, o2, o3)):
        q = g ^ d
        before = pl.ds(pl.multiple_of(jnp.maximum(HELD * q - 8, 0), 8), 8)
        here = pl.ds(pl.multiple_of(HELD * q, HELD), HELD)
        after = pl.ds(pl.multiple_of(jnp.minimum(HELD * q + HELD, ROWS - 8), 8), 8)
        for k in range(LOCAL):
            for p in range(2):
                rows = [start[k, p, at, :] for at in (before, here, after)]
                at = k * 40 + 20 * p
                out[at : at + 20, :] = jnp.concatenate(rows, axis=0)[6:26]

        def clear(first):
            for k in range(LOCAL):
                for p in range(2):
                    at = k * 40 + 20 * p + first
                    out[at : at + 2, :] = jnp.zeros((2, LANES), F32)

        pl.when(q == 0)(functools.partial(clear, 0))
        pl.when(q == GROUPS - 1)(functools.partial(clear, 18))


def pack_fields(ids, mean, kl, even, odd, own, padded, sems):
    g, parity = ids[0], ids[1]
    one = fill_padded(mean, padded.at[0], sems.at[0])
    two = fill_padded(kl, padded.at[pl.ds(1, FIELDS - 1)], sems.at[1])
    one.wait()
    two.wait()
    for m in range(FIELDS):
        for p in range(2):
            own[m, p, 7:27, :] = window(padded, (m, p), g, -2, 20)
    for out, plane in ((even, 1 - parity), (odd, parity)):
        out[0:ROWS, :] = padded[0, plane, 8 : 8 + ROWS, :]
        for m in range(1, FIELDS):
            at = ROWS + 18 * (m - 1)
            out[at : at + 18, :] = own[m, plane, 8:26, :]


def pack_source(ids, source, o0, o1, o2, o3, padded, sem):
    g = ids[0]
    fill_padded(source, padded, sem).wait()
    for d, out in enumerate((o0, o1, o2, o3)):
        for p in range(2):
            for k in range(LOCAL):
                at = k * 36 + 18 * p
                out[at : at + 18, :] = window(padded, (k, p), g ^ d, -1, 18)


def edge(src, k, top, upward):
    low = src[k * 40 + 1 : k * 40 + 19, :]
    high = src[k * 40 + 21 : k * 40 + 39, :]
    return jnp.where(top == upward, high, low)


def pack_near(ids, s0, s1, odd):
    top = ids[1] == 0
    for d, src in enumerate((s0, s1)):
        for k in range(LOCAL):
            at = 18 * (LOCAL * d + k)
            odd[at : at + 18, :] = edge(src, k, top, False)


def pack_far(ids, s0, s1, s2, s3, field_even, field_odd, even, odd):
    top = ids[1] == 0
    for d, src in enumerate((s0, s1, s2, s3)):
        for k in range(LOCAL):
            pos = LOCAL * d + k
            even[18 * pos : 18 * pos + 18, :] = edge(src, k, top, True)
            if pos >= NEAR:
                at = 18 * (pos - NEAR)
                odd[at : at + 18, :] = edge(src, k, top, False)
    even[EDGE:, :] = field_even[...]
    odd[EDGE // 2 :, :] = field_odd[...]


def sides(ids, from_even, from_odd):
    top = ids[1] == 0
    return jnp.where(top, from_odd, from_even), jnp.where(top, from_even, from_odd)


def near_odd(ids, straight, relayed):
    return jnp.where(ids[2] == 1, relayed, straight)


def rows_of(src, plane, lower, upper, count):
    low, high = src[lower : lower + count, :], src[upper : upper + count, :]
    return jnp.where(plane == 0, low, high)


def accumulate(trip, coef, accs, term, visit=None):
    def step(e, carry):
        for lane, acc in enumerate(accs):
            n = e * len(accs) + lane
            m, i, j, c = trip[n], trip[ENTRIES + n], trip[2 * ENTRIES + n], coef[n]
            if visit is not None:
                visit(m, i, c)
            term(acc, m, i, j, c)
        return carry

    lax.fori_loop(0, ENTRIES // len(accs), step, 0, unroll=UNROLL)


def first_inner(
    trip, coef, s0, s1, s2, s3, ae, acc, faces, inverse, vv, nxt, prv, diag
):
    for d, src in enumerate((s0, s1, s2, s3)):
        for k in range(LOCAL):
            pos = LOCAL * d + k
            for p in range(2):
                vv[pos, p, 7:27, :] = src[k * 40 + 20 * p : k * 40 + 20 * p + 20, :]
                mine = vv[pos, p, 8:32, :]
                nxt[pos, p] = lane_next(mine)
                prv[pos, p] = lane_prev(mine)
    for m in range(FIELDS):
        for p in range(2):
            own = ae[m, p, 8:32, :]
            others = (
                ae[m, 1 - p, 8:32, :],
                ae[m, p, 9:33, :], ae[m, p, 7:31, :],
                lane_next(own), lane_prev(own),
            )
            total = None
            for b, other in enumerate(others):
                face = 0.5 * (own + other)
                total = face if total is None else total + face
                faces[m, 2 + b, p] = -face
            faces[m, 0, p] = total
            faces[m, 1, p] = own
    acc[...] = jnp.zeros(acc.shape, F32)

    def term(acc, m, i, j, c):
        for p in range(2):
            total = faces[m, 0, p] * vv[j, p, 8:32, :] + faces[m, 2, p] * vv[j, 1 - p, 8:32, :]
            total += faces[m, 3, p] * vv[j, p, 9:33, :] + faces[m, 4, p] * vv[j, p, 7:31, :]
            total += faces[m, 5, p] * nxt[j, p] + faces[m, 6, p] * prv[j, p]
            acc[i, p] += c * total

    def visit(m, i, c):
        diag[jnp.where(m == 0, i, SLOTS)] = c

    accumulate(trip, coef, (acc,), term, visit)
    for pos in range(SLOTS):
        inverse[pos : pos + 1, :] = 1.0 / jnp.full((1, LANES), diag[pos], F32)


def first_side(odd, trip, coef, ids, inner, faces, inverse, *rest):
    count = 3 if odd else 1
    planes, rest = rest[:count], rest[count:]
    starts, sources, rest = rest[:4], rest[4:8], rest[8:]
    mid, *sends, outer, acc, more, zz, pad = rest
    g = ids[0]
    p = ids[1] if odd else 1 - ids[1]
    if odd:
        near, far, relayed = planes
        base, fields = EDGE // 2, far
    else:
        base, fields = EDGE, planes[0]
    for m in range(FIELDS):
        at = base + ROWS + 18 * (m - 1)
        if m == 0:
            pad[0:8, :] = jnp.zeros((8, LANES), F32)
            pad[8 : 8 + ROWS, :] = fields[base : base + ROWS, :]
            pad[8 + ROWS :, :] = jnp.zeros((8, LANES), F32)
            other = window(pad, (), g, -1, 18)
        else:
            other = fields[at : at + 18, :]
        outer[m, 0:18, :] = 0.5 * (faces[m, 1, p, 0:18, :] + other)
    for pos in range(SLOTS):
        rows = slice(18 * pos, 18 * pos + 18)
        if not odd:
            z = planes[0][rows, :]
        elif pos < NEAR:
            z = near_odd(ids, near[rows, :], relayed[rows, :])
        else:
            z = far[18 * (pos - NEAR) : 18 * (pos - NEAR) + 18, :]
        at = pos % LOCAL * 40 + 1
        zz[pos, 0:18, :] = rows_of(starts[pos // LOCAL], p, at, at + 20, 18) - z
    acc[...] = inner[:, p]
    more[...] = jnp.zeros(more.shape, F32)

    def term(acc, m, i, j, c):
        acc[i] += c * (outer[m] * zz[j])

    accumulate(trip, coef, (acc, more), term)
    row = HELD * g - 1 + lax.broadcasted_iota(jnp.int32, (18, LANES), 0)
    inside = (row >= 0) & (row < ROWS)
    rate = 0.8 / (faces[0, 0, p, 0:18, :] + outer[0, 0:18, :])
    for pos in range(SLOTS):
        at = pos % LOCAL * 36
        first = rows_of(sources[pos // LOCAL], p, at, at + 18, 18)
        first = first - (acc[pos, 0:18, :] + more[pos, 0:18, :])
        at = pos % LOCAL * 40 + 1
        moved = rows_of(starts[pos // LOCAL], p, at, at + 20, 18)
        moved = moved + first * rate * inverse[pos : pos + 1, :]
        moved = jnp.where(inside, moved, 0.0)
        mid[pos, 7:25, :] = moved
        if odd:
            sends[pos // NEAR][pos % NEAR] = moved[1 : 1 + HELD]
        else:
            sends[0][pos] = moved[1 : 1 + HELD]


HERE = slice(1, 1 + HELD)


def in_plane(faces, p, m, j, mine, other, nxt, prv):
    total = faces[m, 0, p, HERE] * mine[j, 8:24, :] + faces[m, 2, p, HERE] * other[j, 8:24, :]
    total += faces[m, 3, p, HERE] * mine[j, 9:25, :] + faces[m, 4, p, HERE] * mine[j, 7:23, :]
    return total + (faces[m, 5, p, HERE] * nxt[j] + faces[m, 6, p, HERE] * prv[j])


def shift_lanes(mine, nxt, prv):
    for pos in range(SLOTS):
        held = mine[pos, 8:24, :]
        nxt[pos] = lane_next(held)
        prv[pos] = lane_prev(held)


def second_even(
    trip, coef, ids, faces, outer, mine, other, met, t0, t1, t2, t3, o0, o1, o2, o3,
    acc, more, zz, nxt, prv,
):
    p = 1 - ids[1]
    shift_lanes(mine, nxt, prv)
    for pos in range(SLOTS):
        zz[pos] = mine[pos, 8:24, :] - met[pos]
    acc[...] = jnp.zeros(acc.shape, F32)
    more[...] = jnp.zeros(more.shape, F32)

    def term(acc, m, i, j, c):
        total = in_plane(faces, p, m, j, mine, other, nxt, prv)
        acc[i] += c * (total + outer[m, HERE] * zz[j])

    accumulate(trip, coef, (acc, more), term)
    for d, (src, out) in enumerate(((t0, o0), (t1, o1), (t2, o2), (t3, o3))):
        for k in range(LOCAL):
            pos = LOCAL * d + k
            out[k, 0] = mine[pos, 8:24, :]
            out[k, 1] = other[pos, 8:24, :]
            at = k * 36 + 1
            out[k, 2] = rows_of(src, p, at, at + 18, HELD) - (acc[pos] + more[pos])


def second_inner(trip, coef, ids, faces, mine, other, acc, more, nxt, prv):
    p = ids[1]
    shift_lanes(mine, nxt, prv)
    acc[...] = jnp.zeros(acc.shape, F32)
    more[...] = jnp.zeros(more.shape, F32)

    def term(acc, m, i, j, c):
        acc[i] += c * in_plane(faces, p, m, j, mine, other, nxt, prv)

    accumulate(trip, coef, (acc, more), term)


def second_odd(
    trip, coef, ids, inner, extra, outer, mine, near, far, relayed, t0, t1, t2, t3,
    o0, o1, o2, o3, acc, more, zz,
):
    p = ids[1]
    for pos in range(SLOTS):
        z = near_odd(ids, near[pos], relayed[pos]) if pos < NEAR else far[pos - NEAR]
        zz[pos] = mine[pos, 8:24, :] - z
    acc[...] = inner[...]
    more[...] = extra[...]

    def term(acc, m, i, j, c):
        acc[i] += c * (outer[m, HERE] * zz[j])

    accumulate(trip, coef, (acc, more), term)
    for d, (src, out) in enumerate(((t0, o0), (t1, o1), (t2, o2), (t3, o3))):
        for k in range(LOCAL):
            pos = LOCAL * d + k
            at = k * 36 + 1
            out[k] = rows_of(src, p, at, at + 18, HELD) - (acc[pos] + more[pos])


def final_rates(ids, mean, far, ev, rate, pad):
    below, above = sides(ids, ev[EDGE : EDGE + ROWS, :], far[EDGE // 2 : EDGE // 2 + ROWS, :])
    pad[0:8, :] = jnp.zeros((8, LANES), F32)
    pad[8 + ROWS :, :] = jnp.zeros((8, LANES), F32)
    for p in range(2):
        own = mean[p]
        pad[8 : 8 + ROWS, :] = own
        others = (
            above if p else mean[1], mean[0] if p else below,
            pad[9 : 9 + ROWS, :], pad[7 : 7 + ROWS, :],
            lane_next(own), lane_prev(own),
        )
        total = None
        for other in others:
            face = 0.5 * (own + other)
            total = face if total is None else total + face
        rate[p] = 0.8 / total


def second_sweep(ids, rate, inverse, m0, m1, m2, m3, r0, r1, r2, r3, smoothed, residual):
    g, parity = ids[0], ids[1]
    for d, (mid, res) in enumerate(((m0, r0), (m1, r1), (m2, r2), (m3, r3))):
        rows = pl.ds(pl.multiple_of(HELD * (g ^ d), HELD), HELD)
        for p in (0, 1):
            plane = parity if p else 1 - parity
            here = rate[plane, rows, :]
            for k in range(LOCAL):
                left = res[k] if p else mid[k, 2]
                residual[k, plane, rows, :] = left
                smoothed[k, plane, rows, :] = mid[k, p] + left * here * inverse[k : k + 1, :]


def body(start_field, source, mean_field, kl_fields, triples, coef):
    g = lax.axis_index("mode").astype(jnp.int32)
    slab = lax.axis_index("space").astype(jnp.int32)
    ids = jnp.stack([g, slab % 2, ((slab % 4 == 0) | (slab % 4 == 3)).astype(jnp.int32)])
    count = lax.axis_size("space")
    def both(pairs):
        return [pair for a, b in pairs for pair in ((a, b), (b, a))]

    evens = both([(i, i + 1) for i in range(0, count, 2)])
    odds = both([(i, i + 1) for i in range(1, count - 1, 2)])
    inner = [(i + 1, i + 2) for i in range(0, count, 4)]
    hops = both(inner + [(i, i + 3) for i in range(0, count, 4)])
    relay = [(i, i + 4) for i in range(0, count - 4, 4)]
    relay += [(i + 7, i + 3) for i in range(0, count - 4, 4)]

    def meet(x, pairs):
        return lax.ppermute(x, "space", pairs)

    def trade(parts):
        return [parts[0]] + [
            lax.ppermute(parts[d], "mode", [(i, i ^ d) for i in range(GROUPS)])
            for d in range(1, GROUPS)
        ]

    sends = pl.pallas_call(
        pack_start,
        out_shape=[shape(360, LANES)] * 4,
        in_specs=[SMEM, VMEM],
        out_specs=[VMEM] * 4,
        name="pack_start",
        **PARAMS,
    )(ids, start_field)
    starts = trade(sends)
    near = pl.pallas_call(
        pack_near,
        out_shape=shape(EDGE // 2, LANES),
        in_specs=[SMEM] + [VMEM] * 2,
        out_specs=VMEM,
        name="pack_near",
        **PARAMS,
    )(ids, *starts[:2])
    mean_late, kl_late, source, near = lax.optimization_barrier(
        (mean_field, kl_fields, source, near)
    )
    near = meet(near, hops)
    *parts, starts[3] = lax.optimization_barrier((
        *pl.pallas_call(
            pack_source,
            out_shape=[shape(324, LANES)] * 4,
            in_specs=[SMEM, HBM],
            out_specs=[VMEM] * 4,
            scratch_shapes=[
                pltpu.VMEM((LOCAL, 2, ROWS + 16, LANES), F32), pltpu.SemaphoreType.DMA
            ],
            name="pack_source",
            **PARAMS,
        )(ids, source),
        starts[3],
    ))
    sources = trade(parts)
    triples, starts[2], sources[1], near = lax.optimization_barrier(
        (triples, starts[2], sources[1], near)
    )
    modes = triples[:, 1:]
    at = LOCAL * ((modes // LOCAL) ^ g) + modes % LOCAL
    trip = jnp.concatenate([triples[:, 0], at[:, 0], at[:, 1]])
    *fields, own_fields = pl.pallas_call(
        pack_fields,
        out_shape=[shape(EDGE_FIELDS, LANES)] * 2 + [shape(FIELDS, 2, 40, LANES)],
        in_specs=[SMEM, HBM, HBM],
        out_specs=[VMEM] * 3,
        scratch_shapes=[
            pltpu.VMEM((FIELDS, 2, ROWS + 16, LANES), F32),
            pltpu.SemaphoreType.DMA((2,)),
        ],
        name="pack_fields",
        **PARAMS,
    )(ids, mean_late, kl_late)
    even, odd = pl.pallas_call(
        pack_far,
        out_shape=[shape(EDGE + EDGE_FIELDS, LANES), shape(EDGE // 2 + EDGE_FIELDS, LANES)],
        in_specs=[SMEM] + [VMEM] * 6,
        out_specs=[VMEM] * 2,
        name="pack_far",
        **PARAMS,
    )(ids, *starts, *fields)
    edges = (near, meet(odd, odds), meet(even, evens))
    relayed = meet(near, relay)
    acc, faces, inverse = pl.pallas_call(
        first_inner,
        out_shape=[
            shape(SLOTS, 2, 24, LANES), shape(FIELDS, 7, 2, 24, LANES), shape(SLOTS, LANES)
        ],
        in_specs=[SMEM] * 2 + [VMEM] * 5,
        out_specs=[VMEM] * 3,
        scratch_shapes=[
            pltpu.VMEM((SLOTS, 2, 40, LANES), F32),
            pltpu.VMEM((SLOTS, 2, 24, LANES), F32),
            pltpu.VMEM((SLOTS, 2, 24, LANES), F32),
            pltpu.SMEM((SLOTS + 1,), F32),
        ],
        cost_estimate=COST,
        name="first_inner",
        **PARAMS,
    )(trip, coef, *starts, own_fields)
    def side(odd, planes, sends):
        operands = (trip, coef, ids, acc, faces, inverse, *planes, *starts, *sources)
        return pl.pallas_call(
            functools.partial(first_side, odd),
            out_shape=[shape(SLOTS, 32, LANES)]
            + [shape(SLOTS // sends, HELD, LANES)] * sends
            + [shape(FIELDS, 24, LANES)],
            in_specs=[SMEM] * 3 + [VMEM] * (len(operands) - 3),
            out_specs=[VMEM] * (2 + sends),
            scratch_shapes=[pltpu.VMEM((SLOTS, 24, LANES), F32)] * 3
            + [pltpu.VMEM((ROWS + 16, LANES), F32)],
            cost_estimate=SIDE_COST,
            name="first_odd" if odd else "first_even",
            **PARAMS,
        )(*operands)

    near, far, even = edges
    mid_even, even, outer_even = side(False, (even,), 1)
    even = meet(even, evens)
    mid_odd, odd_a, odd_b, outer_odd = side(True, (near, far, relayed), 2)
    near = meet(odd_a, hops)
    far = meet(odd_b, odds)
    relayed = meet(near, relay)
    held = pltpu.VMEM((SLOTS, HELD, LANES), F32)
    mids = trade(pl.pallas_call(
        second_even,
        out_shape=[shape(LOCAL, 3, HELD, LANES)] * 4,
        in_specs=[SMEM] * 3 + [VMEM] * 9,
        out_specs=[VMEM] * 4,
        scratch_shapes=[held] * 5,
        cost_estimate=COST,
        name="second_even",
        **PARAMS,
    )(trip, coef, ids, faces, outer_even, mid_even, mid_odd, even, *sources))
    acc = pl.pallas_call(
        second_inner,
        out_shape=[shape(SLOTS, HELD, LANES)] * 2,
        in_specs=[SMEM] * 3 + [VMEM] * 3,
        out_specs=[VMEM] * 2,
        scratch_shapes=[held] * 2,
        cost_estimate=COST,
        name="second_inner",
        **PARAMS,
    )(trip, coef, ids, faces, mid_odd, mid_even)
    lefts = trade(pl.pallas_call(
        second_odd,
        out_shape=[shape(LOCAL, HELD, LANES)] * 4,
        in_specs=[SMEM] * 3 + [VMEM] * 11,
        out_specs=[VMEM] * 4,
        scratch_shapes=[held] * 3,
        name="second_odd",
        **PARAMS,
    )(trip, coef, ids, *acc, outer_odd, mid_odd, near, far, relayed, *sources))
    rate = pl.pallas_call(
        final_rates,
        out_shape=shape(2, ROWS, LANES),
        in_specs=[SMEM] + [VMEM] * 3,
        out_specs=VMEM,
        scratch_shapes=[pltpu.VMEM((ROWS + 16, LANES), F32)],
        name="final_rates",
        **PARAMS,
    )(ids, mean_field, *edges[1:])
    smoothed, residual = pl.pallas_call(
        second_sweep,
        out_shape=[shape(LOCAL, 2, ROWS, LANES)] * 2,
        in_specs=[SMEM] + [VMEM] * 10,
        out_specs=[VMEM] * 2,
        name="second_sweep",
        **PARAMS,
    )(ids, rate, inverse, *mids, *lefts)
    return (smoothed, residual)


def solution(mesh):
    return jax.shard_map(
        body,
        mesh=mesh,
        in_specs=(
            P("mode", "space", None, None),
            P("mode", "space", None, None),
            P("space", None, None),
            P(None, "space", None, None),
            P(),
            P(),
        ),
        out_specs=(P("mode", "space", None, None), P("mode", "space", None, None)),
        check_vma=False,
    )
```
